512 devices in a mesh: fsdp: 64 (over y, x, core), dp: 8 (over z).
Axes of the slice: x: 4, y: 8, z: 8, core: 2. Of those that a mesh axis runs over, the one named last changes fastest.
Arguments:
- grads: bfloat16 [8, 64, 1024, 1024], P('dp', None, 'fsdp'), may hold values from -7 to 7
- assign: int32 [64], replicated, may hold values from 0 to 63, each once
- left_factor: float32 [64, 1024, 1024], P('fsdp', 'dp'), may hold values from -1 to 4, as said below
- right_factor: float32 [64, 1024, 1024], P('fsdp', 'dp'), may hold values from -1 to 4, as said below
- left_root: bfloat16 [64, 1024, 1024], P('fsdp', 'dp'), may hold values from -1 to 3, as said below
- right_root: bfloat16 [64, 1024, 1024], P('fsdp', 'dp'), may hold values from -1 to 3, as said below
Outputs:
- update: bfloat16 [64, 1024, 1024], P(None, 'fsdp', 'dp')
- left_new: float32 [64, 1024, 1024], P('fsdp', 'dp')
- right_new: float32 [64, 1024, 1024], P('fsdp', 'dp')
The draws below stay inside these ranges and needn't reach their ends.
Inputs may be any that keep to these rules, and one draw needn't show every extreme that they name: `assign`: a permutation: each owner holds exactly one block. `left_factor`: each owner's matrix is symmetric. `right_factor`: each owner's matrix is symmetric. `left_root`: each owner's matrix is symmetric. `right_root`: each owner's matrix is symmetric.
All inputs are finite; a program needn't handle non-finite values.
Results may differ from the reference program's by a relative error of at most 0.001.
Values may be sent and summed in bfloat16 or wider, within the bound.
No kernel may reach another device: no remote copies, remote signals or barrier semaphores. Data moves between devices by JAX's collectives and lax.ppermute only.
A program may use at most 64 MiB of HBM per device.

```python
import jax
import jax.numpy as jnp
from jax import lax

BLK = 1024
NBLK = 64
N_FSDP = 64
N_DP = 8


def log_spread(key, shape, low, high):
    return low * (high / low) ** jax.random.uniform(key, shape, jnp.float32)


def make_symmetric(noise, diag_key, low, high, off_scale):
    count = noise.shape[-1]
    mixed = (noise + jnp.swapaxes(noise, 1, 2)) * off_scale
    identity = (jnp.arange(count)[:, None] == jnp.arange(count)[None, :]).astype(jnp.float32)
    diagonal = log_spread(diag_key, noise.shape[:2], low, high)
    return mixed * (1.0 - identity) + diagonal[:, :, None] * identity


def draw_grads(key, part):
    key = jax.random.fold_in(key, 1)
    row_key, col_key, own_key = jax.random.split(key, 3)
    row_scale = log_spread(row_key, (NBLK, BLK), 0.3, 3.0)
    col_scale = log_spread(col_key, (NBLK, BLK), 0.3, 3.0)
    values = jnp.clip(jax.random.normal(own_key, (N_DP, NBLK, BLK, BLK), jnp.float32), -6.0, 6.0)
    period = BLK // N_FSDP
    ramp_scale = 3.0 ** ((jnp.arange(BLK) % period).astype(jnp.float32) / period)
    scaled = 0.04 * values * (row_scale * ramp_scale)[None, :, :, None] * col_scale[None, :, None, :]
    return scaled.astype(jnp.bfloat16)


def factor_noise(key):
    return jnp.clip(jax.random.normal(key, (N_FSDP, BLK, BLK), jnp.float32), -6.0, 6.0)


def draw_left_factor(key, part):
    key = jax.random.fold_in(key, 2)
    noise_key, diag_key = jax.random.split(key)
    return make_symmetric(factor_noise(noise_key), diag_key, 0.5, 3.0, 0.6 * (2 * BLK) ** (-0.5))


def draw_right_factor(key, part):
    key = jax.random.fold_in(key, 3)
    noise_key, diag_key = jax.random.split(key)
    return make_symmetric(factor_noise(noise_key), diag_key, 0.5, 3.0, 0.6 * (2 * BLK) ** (-0.5))


def draw_left_root(key, part):
    key = jax.random.fold_in(key, 4)
    noise_key, diag_key = jax.random.split(key)
    return make_symmetric(factor_noise(noise_key), diag_key, 0.5, 2.0, 0.5 * (2 * BLK) ** (-0.5)).astype(jnp.bfloat16)


def draw_right_root(key, part):
    key = jax.random.fold_in(key, 5)
    noise_key, diag_key = jax.random.split(key)
    return make_symmetric(factor_noise(noise_key), diag_key, 0.5, 2.0, 0.5 * (2 * BLK) ** (-0.5)).astype(jnp.bfloat16)


def setup_inputs(seed: int = 0) -> dict:
    splits = jax.random.split(jax.random.key(seed), 7)
    grads = draw_grads(jax.random.fold_in(splits[6], 71), 0)
    assign = jax.random.permutation(splits[1], NBLK).astype(jnp.int32)
    left_factor = draw_left_factor(jax.random.fold_in(splits[6], 71), 0)
    right_factor = draw_right_factor(jax.random.fold_in(splits[6], 71), 0)
    left_root = draw_left_root(jax.random.fold_in(splits[6], 71), 0)
    right_root = draw_right_root(jax.random.fold_in(splits[6], 71), 0)
    return {"grads": grads, "assign": assign, "left_factor": left_factor, "right_factor": right_factor, "left_root": left_root, "right_root": right_root}


DECAY_RATE = 0.999
EPSILON = 1e-06
PRECISE = lax.Precision.HIGHEST

def reference(grads, assign, left_factor, right_factor, left_root, right_root):
    owners = jnp.arange(N_FSDP, dtype=jnp.int32)
    numbers = jnp.arange(NBLK, dtype=jnp.int32)
    matches = (assign[:, None] == owners[None, :]).astype(jnp.int32)
    held = lax.optimization_barrier(jnp.sum(numbers[:, None] * matches, axis=0)).astype(jnp.int32)

    def one_owner(owner_id):
        block_grads = jnp.take(grads, held[owner_id], axis=1).astype(jnp.float32)
        summed = lax.optimization_barrier(jnp.sum(block_grads, axis=0))
        left_out = DECAY_RATE * left_factor[owner_id] + (1.0 - DECAY_RATE) * jnp.dot(summed, summed.T, precision=PRECISE)
        right_out = DECAY_RATE * right_factor[owner_id] + (1.0 - DECAY_RATE) * jnp.dot(summed.T, summed, precision=PRECISE)
        sectioned = jnp.dot(left_root[owner_id].astype(jnp.float32), summed, precision=PRECISE)
        conditioned = jnp.dot(sectioned, right_root[owner_id].astype(jnp.float32), precision=PRECISE)
        graft = jnp.sqrt((jnp.sum(summed * summed) + EPSILON) / (jnp.sum(conditioned * conditioned) + EPSILON))
        rounded = (conditioned * graft).astype(jnp.bfloat16)
        return (rounded, left_out, right_out)
    per_owner, left_new, right_new = lax.map(one_owner, owners)
    return (jnp.take(per_owner, assign, axis=0), left_new, right_new)
```

```python
import jax
import jax.numpy as jnp
from jax import lax
from jax.sharding import PartitionSpec as P

DECAY_RATE = 0.999
EPSILON = 1e-06
PRECISE = lax.Precision.HIGHEST
STEPS = 128.0
TOP = 32767.0
FLOOR = 1e-30


def code_of(peak):
    return jnp.ceil(jnp.log2(jnp.maximum(peak, FLOOR)) * STEPS)


def scale_of(code):
    return jnp.exp2(code * (1.0 / STEPS)) * (1.0 / TOP)


def body(grads, assign, left_factor, right_factor, left_root, right_root):
    fsdp_size = lax.axis_size("fsdp")
    dp_size = lax.axis_size("dp")
    blocks = grads.shape[1]
    shard_rows = grads.shape[2]
    width = grads.shape[3]
    col_width = width // dp_size
    member_id = lax.axis_index("dp")
    owners = jnp.arange(fsdp_size, dtype=jnp.int32)
    numbers = jnp.arange(blocks, dtype=jnp.int32)
    matches = (assign[:, None] == owners[None, :]).astype(jnp.int32)
    held = jnp.sum(numbers[:, None] * matches, axis=0)
    left_full = lax.all_gather(left_root[0], "dp", axis=0, tiled=True)
    outgoing = jnp.take(grads[0], held, axis=0, mode="clip")
    outgoing = outgoing.reshape(fsdp_size, shard_rows, dp_size, col_width).transpose(0, 2, 1, 3)
    outgoing = outgoing.reshape(fsdp_size * dp_size, shard_rows, col_width)
    arrived = lax.all_to_all(outgoing, ("fsdp", "dp"), split_axis=0, concat_axis=0, tiled=True)
    terms = arrived.reshape(fsdp_size, dp_size, shard_rows, col_width).astype(jnp.float32)
    own = jnp.sum(terms, axis=1).reshape(width, col_width)
    codes = code_of(jnp.max(jnp.abs(own), axis=1))
    units = jnp.clip(jnp.round(own / scale_of(codes)[:, None]), -TOP, TOP).astype(jnp.int16)
    packed = jnp.concatenate([units, codes.astype(jnp.int16).reshape(-1, col_width)], axis=0)
    spread = lax.all_gather(packed, "dp", axis=0)
    scales = scale_of(spread[:, width:].reshape(dp_size, width).astype(jnp.float32))
    slabs = spread[:, :width].astype(jnp.float32) * scales[:, :, None]
    gathered = slabs.transpose(1, 0, 2).reshape(width, width)
    contract_cols = (((1,), (1,)), ((), ()))
    contract_rows = (((0,), (0,)), ((), ()))
    own_rows = lax.dynamic_slice_in_dim(gathered, member_id * col_width, col_width, 0)
    own_cols = lax.dynamic_slice_in_dim(gathered, member_id * col_width, col_width, 1)
    right_cols = lax.dot_general(
        gathered, right_root[0].astype(jnp.float32), contract_cols, precision=PRECISE
    )
    conditioned = jnp.dot(left_full.astype(jnp.float32), right_cols, precision=PRECISE)
    block_square = jnp.sum(gathered * gathered)
    shaped_square = lax.psum(jnp.sum(conditioned * conditioned), "dp")
    graft = jnp.sqrt((block_square + EPSILON) / (shaped_square + EPSILON))
    rounded = (conditioned * graft).astype(jnp.bfloat16).reshape(fsdp_size, shard_rows, col_width)
    returned = lax.all_to_all(rounded, "fsdp", split_axis=0, concat_axis=0, tiled=True)
    left_out = DECAY_RATE * left_factor[0] + (1.0 - DECAY_RATE) * lax.dot_general(
        own_rows, gathered, contract_cols, precision=PRECISE
    )
    right_out = DECAY_RATE * right_factor[0] + (1.0 - DECAY_RATE) * lax.dot_general(
        own_cols, gathered, contract_rows, precision=PRECISE
    )
    update = jnp.take(returned, assign, axis=0, mode="clip")
    return (update, left_out[None], right_out[None])


def solution(mesh):
    placed = (
        P("dp", None, "fsdp", None),
        P(),
        P("fsdp", "dp", None),
        P("fsdp", "dp", None),
        P("fsdp", "dp", None),
        P("fsdp", "dp", None),
    )
    return jax.shard_map(
        body,
        mesh=mesh,
        in_specs=placed,
        out_specs=(P(None, "fsdp", "dp"), P("fsdp", "dp", None), P("fsdp", "dp", None)),
        check_vma=False,
    )
```

```python
import functools

import jax
import jax.numpy as jnp
from jax import lax
from jax.experimental import pallas as pl
from jax.experimental.pallas import tpu as pltpu
from jax.sharding import PartitionSpec as P

DECAY_RATE = 0.999
EPSILON = 1e-06
STEPS = 90.0
TOP = 32767.0
FLOOR = 1e-30
CODES = 16
MIB = 1 << 20


def vmem():
    return pl.BlockSpec(memory_space=pltpu.VMEM)


def anywhere():
    return pl.BlockSpec(memory_space=pl.ANY)


def cost(flops, moved):
    return pl.CostEstimate(flops=flops, bytes_accessed=moved, transcendentals=0)


def send_kernel(dp_size, assign_ref, grads_ref, out_ref, held, turned, in_sems, out_sem):
    blocks = grads_ref.shape[0]
    col_width = grads_ref.shape[2] // dp_size
    chunks = in_sems.shape[0]
    chunk = blocks // chunks
    loads = [
        pltpu.make_async_copy(
            grads_ref.at[pl.ds(c * chunk, chunk)], held.at[pl.ds(c * chunk, chunk)], in_sems.at[c]
        )
        for c in range(chunks)
    ]
    for load in loads:
        load.start()
    for c in range(chunks):
        loads[c].wait()

        def turn(b, carry):
            for k in range(dp_size):
                turned[b, k] = held[b, :, pl.ds(k * col_width, col_width)]
            pltpu.make_async_copy(turned.at[b], out_ref.at[assign_ref[b]], out_sem).start()
            return carry

        lax.fori_loop(c * chunk, (c + 1) * chunk, turn, 0)
    pltpu.make_async_copy(turned, out_ref, out_sem).wait()


def send(assign, grads, dp_size):
    blocks, rows, width = grads.shape
    shape = (blocks, dp_size, rows, width // dp_size)
    return pl.pallas_call(
        functools.partial(send_kernel, dp_size),
        out_shape=jax.ShapeDtypeStruct(shape, grads.dtype),
        in_specs=[pl.BlockSpec(memory_space=pltpu.SMEM), anywhere()],
        out_specs=anywhere(),
        scratch_shapes=[
            pltpu.VMEM(grads.shape, grads.dtype),
            pltpu.VMEM(shape, grads.dtype),
            pltpu.SemaphoreType.DMA((4,)),
            pltpu.SemaphoreType.DMA,
        ],
        compiler_params=pltpu.CompilerParams(vmem_limit_bytes=16 * MIB),
        cost_estimate=cost(0, 2 * grads.size * 2),
        name="send",
    )(assign, grads)


def scale_of(code):
    return jnp.exp(code * (1.0 / STEPS)) * (1.0 / TOP)


def fold_kernel(arrived_ref, packed_ref):
    shards, replicas, rows, width = arrived_ref.shape
    group = shards // CODES
    codes = []
    for g in range(CODES):
        terms = arrived_ref[pl.ds(g * group, group)].astype(jnp.float32)
        total = jnp.sum(terms, axis=1).reshape(group * rows, width)
        peak = jnp.maximum(jnp.max(jnp.abs(total), axis=0, keepdims=True), FLOOR)
        code = jnp.ceil(jnp.log(peak) * STEPS)
        units = jnp.floor(total * (1.0 / scale_of(code)) + 0.5)
        units = jnp.clip(units, -TOP, TOP).astype(jnp.int32).astype(jnp.int16)
        packed_ref[pl.ds(g * group * rows, group * rows), :] = units
        codes.append(code)
    codes = jnp.concatenate(codes, axis=0).astype(jnp.int32).astype(jnp.int16)
    packed_ref[pl.ds(shards * rows, CODES), :] = codes


def fold(arrived):
    shards, replicas, rows, width = arrived.shape
    return pl.pallas_call(
        fold_kernel,
        out_shape=jax.ShapeDtypeStruct((shards * rows + CODES, width), jnp.int16),
        in_specs=[vmem()],
        out_specs=vmem(),
        compiler_params=pltpu.CompilerParams(vmem_limit_bytes=16 * MIB),
        cost_estimate=cost(arrived.size, 2 * arrived.size),
        name="fold",
    )(arrived)


def unpack(spread_ref, k, high, low):
    width = spread_ref.shape[2]
    size = spread_ref.shape[1] - CODES
    rows = size // CODES
    columns = pl.ds(k * width, width)
    scales = scale_of(spread_ref[k, pl.ds(size, CODES), :].astype(jnp.int32).astype(jnp.float32))
    square = jnp.zeros((8, width), jnp.float32)
    for g in range(CODES):
        here = pl.ds(g * rows, rows)
        units = spread_ref[k, here, :].astype(jnp.int32).astype(jnp.float32)
        values = units * scales[g : g + 1]
        upper = values.astype(jnp.bfloat16)
        high[here, columns] = upper
        low[here, columns] = (values - upper.astype(jnp.float32)).astype(jnp.bfloat16)
        square = square + jnp.sum((values * values).reshape(rows // 8, 8, width), axis=0)
    return square


NT = (((1,), (1,)), ((), ()))
NN = (((1,), (0,)), ((), ()))


def dot(a, b, dims):
    return lax.dot_general(a, b, dims, preferred_element_type=jnp.float32)


def shape_kernel(spread_ref, left_ref, right_ref, out_ref, squares_ref, total_ref, high, low, mid):
    slabs = spread_ref.shape[0]
    size, width = out_ref.shape
    tile = 256
    square = jnp.zeros((8, width), jnp.float32)
    for k in range(slabs):
        square = square + unpack(spread_ref, k, high, low)
    total_ref[...] = square

    def right_step(t, carry):
        rows = pl.ds(pl.multiple_of(t * tile, tile), tile)
        part = dot(high[rows, :], right_ref[...], NT) + dot(low[rows, :], right_ref[...], NT)
        upper = part.astype(jnp.bfloat16)
        mid[rows, pl.ds(0, width)] = upper
        mid[rows, pl.ds(width, width)] = (part - upper.astype(jnp.float32)).astype(jnp.bfloat16)
        return carry

    lax.fori_loop(0, size // tile, right_step, 0)

    def left_step(t, square):
        rows = pl.ds(pl.multiple_of(t * tile, tile), tile)
        both = dot(left_ref[rows, :], mid[...], NN)
        part = both[:, :width] + both[:, width:]
        out_ref[rows, :] = part
        return square + jnp.sum((part * part).reshape(tile // 8, 8, width), axis=0)

    square = lax.fori_loop(0, size // tile, left_step, jnp.zeros((8, width), jnp.float32))
    for k in range(slabs):
        squares_ref[k] = square


def shape(spread, left, right):
    slabs, _, width = spread.shape
    size = left.shape[0]
    return pl.pallas_call(
        shape_kernel,
        out_shape=(
            jax.ShapeDtypeStruct((size, width), jnp.float32),
            jax.ShapeDtypeStruct((slabs, 8, width), jnp.float32),
            jax.ShapeDtypeStruct((8, width), jnp.float32),
        ),
        in_specs=[vmem()] * 3,
        out_specs=(vmem(),) * 3,
        scratch_shapes=[
            pltpu.VMEM((size, size), jnp.bfloat16),
            pltpu.VMEM((size, size), jnp.bfloat16),
            pltpu.VMEM((size, 2 * width), jnp.bfloat16),
        ],
        compiler_params=pltpu.CompilerParams(vmem_limit_bytes=24 * MIB),
        cost_estimate=cost(8 * size * size * width, 6 * size * size),
        name="shape",
    )(spread, left, right)


def graft_kernel(shaped_ref, squares_ref, total_ref, out_ref):
    def whole(x):
        return jnp.sum(jnp.sum(x, axis=0, keepdims=True), axis=1, keepdims=True)

    shaped_square = whole(jnp.sum(squares_ref[...], axis=0))
    block_square = whole(total_ref[...])
    ratio = jnp.sqrt((block_square + EPSILON) / (shaped_square + EPSILON))
    out_ref[...] = (shaped_ref[...] * ratio).astype(jnp.bfloat16)


def graft(shaped, squares, total):
    return pl.pallas_call(
        graft_kernel,
        out_shape=jax.ShapeDtypeStruct(shaped.shape, jnp.bfloat16),
        in_specs=[vmem()] * 3,
        out_specs=vmem(),
        compiler_params=pltpu.CompilerParams(vmem_limit_bytes=8 * MIB),
        cost_estimate=cost(shaped.size, 6 * shaped.size),
        name="graft",
    )(shaped, squares, total)


def stats_kernel(place_ref, spread_ref, left_ref, right_ref, left_out, right_out, high, low, turned):
    slabs = spread_ref.shape[0]
    rows, size = left_ref.shape
    tile = 256
    for k in range(slabs):
        unpack(spread_ref, k, high, low)
    own = pl.ds(pl.multiple_of(place_ref[0] * rows, rows), rows)
    turned[pl.ds(0, rows), :] = high[:, own].T
    turned[pl.ds(rows, rows), :] = low[:, own].T

    def step(t, carry):
        here = pl.ds(pl.multiple_of(t * tile, tile), tile)
        part = dot(high[own, :], high[here, :], NT)
        part += dot(low[own, :], high[here, :], NT)
        part += dot(high[own, :], low[here, :], NT)
        left_out[:, here] = DECAY_RATE * left_ref[:, here] + (1.0 - DECAY_RATE) * part
        both = dot(turned[...], high[:, here], NN)
        part = both[:rows] + both[rows:] + dot(turned[pl.ds(0, rows), :], low[:, here], NN)
        right_out[:, here] = DECAY_RATE * right_ref[:, here] + (1.0 - DECAY_RATE) * part
        return carry

    lax.fori_loop(0, size // tile, step, 0)


def stats(place, spread, left, right):
    rows, size = left.shape
    return pl.pallas_call(
        stats_kernel,
        out_shape=(jax.ShapeDtypeStruct(left.shape, left.dtype),) * 2,
        in_specs=[pl.BlockSpec(memory_space=pltpu.SMEM)] + [vmem()] * 3,
        out_specs=(vmem(),) * 2,
        scratch_shapes=[
            pltpu.VMEM((size, size), jnp.bfloat16),
            pltpu.VMEM((size, size), jnp.bfloat16),
            pltpu.VMEM((2 * rows, size), jnp.bfloat16),
        ],
        compiler_params=pltpu.CompilerParams(vmem_limit_bytes=24 * MIB),
        cost_estimate=cost(12 * size * size * rows, 6 * size * size),
        name="stats",
    )(place, spread, left, right)


def body(grads, assign, left_factor, right_factor, left_root, right_root):
    fsdp_size = lax.axis_size("fsdp")
    dp_size = lax.axis_size("dp")
    shard_rows = grads.shape[2]
    width = grads.shape[3]
    col_width = width // dp_size
    place = lax.axis_index("dp").astype(jnp.int32).reshape(1)
    left_full = lax.all_gather(left_root[0], "dp", axis=0, tiled=True)
    outgoing = send(assign, grads[0], dp_size)
    outgoing = outgoing.reshape(fsdp_size * dp_size, shard_rows, col_width)
    arrived = lax.all_to_all(outgoing, ("fsdp", "dp"), split_axis=0, concat_axis=0, tiled=True)
    packed = fold(arrived.reshape(fsdp_size, dp_size, shard_rows, col_width))
    spread = lax.all_gather(packed, "dp", axis=0)
    shaped, squares, total = shape(spread, left_full, right_root[0])
    squares = lax.all_to_all(squares, "dp", split_axis=0, concat_axis=0, tiled=True)
    rounded = graft(shaped, squares, total).reshape(fsdp_size, shard_rows, col_width)
    rounded, spread = lax.optimization_barrier((rounded, spread))
    returned = lax.all_to_all(rounded, "fsdp", split_axis=0, concat_axis=0, tiled=True)
    left_out, right_out = stats(place, spread, left_factor[0], right_factor[0])
    update = jnp.take(returned, assign, axis=0, mode="clip")
    return (update, left_out[None], right_out[None])


def solution(mesh):
    placed = (
        P("dp", None, "fsdp", None),
        P(),
        P("fsdp", "dp", None),
        P("fsdp", "dp", None),
        P("fsdp", "dp", None),
        P("fsdp", "dp", None),
    )
    return jax.shard_map(
        body,
        mesh=mesh,
        in_specs=placed,
        out_specs=(P(None, "fsdp", "dp"), P("fsdp", "dp", None), P("fsdp", "dp", None)),
        check_vma=False,
    )
```

```python
import functools

import jax
import jax.numpy as jnp
from jax import lax
from jax.experimental import pallas as pl
from jax.experimental.pallas import tpu as pltpu
from jax.sharding import PartitionSpec as P

DECAY_RATE = 0.999
EPSILON = 1e-06
STEPS = 90.0
TOP = 32767.0
FLOOR = 1e-30
CODES = 16
BITS = (64, 32, 16, 8, 4, 2, 1)
MIB = 1 << 20


def vmem():
    return pl.BlockSpec(memory_space=pltpu.VMEM)


def anywhere():
    return pl.BlockSpec(memory_space=pl.ANY)


def cost(flops, moved):
    return pl.CostEstimate(flops=flops, bytes_accessed=moved, transcendentals=0)


def send_kernel(dp_size, assign_ref, grads_ref, out_ref, held, turned, in_sems, out_sem):
    blocks = grads_ref.shape[0]
    col_width = grads_ref.shape[2] // dp_size
    chunks = in_sems.shape[0]
    chunk = blocks // chunks
    loads = [
        pltpu.make_async_copy(
            grads_ref.at[pl.ds(c * chunk, chunk)], held.at[pl.ds(c * chunk, chunk)], in_sems.at[c]
        )
        for c in range(chunks)
    ]
    for load in loads:
        load.start()
    for c in range(chunks):
        loads[c].wait()

        def turn(b, carry):
            for k in range(dp_size):
                turned[b, k] = held[b, :, pl.ds(k * col_width, col_width)]
            pltpu.make_async_copy(turned.at[b], out_ref.at[assign_ref[b]], out_sem).start()
            return carry

        lax.fori_loop(c * chunk, (c + 1) * chunk, turn, 0, unroll=True)
    pltpu.make_async_copy(turned, out_ref, out_sem).wait()


def send(assign, grads, dp_size):
    blocks, rows, width = grads.shape
    shape = (blocks, dp_size, rows, width // dp_size)
    return pl.pallas_call(
        functools.partial(send_kernel, dp_size),
        out_shape=jax.ShapeDtypeStruct(shape, grads.dtype),
        in_specs=[pl.BlockSpec(memory_space=pltpu.SMEM), anywhere()],
        out_specs=anywhere(),
        scratch_shapes=[
            pltpu.VMEM(grads.shape, grads.dtype),
            pltpu.VMEM(shape, grads.dtype),
            pltpu.SemaphoreType.DMA((8,)),
            pltpu.SemaphoreType.DMA,
        ],
        compiler_params=pltpu.CompilerParams(vmem_limit_bytes=60 * MIB),
        cost_estimate=cost(0, 2 * grads.size * 2),
        name="send",
    )(assign, grads)


def scale_of(code):
    return jnp.exp(code * (1.0 / STEPS)) * (1.0 / TOP)


def fold_kernel(arrived_ref, root_ref, packed_ref):
    shards, replicas, rows, width = arrived_ref.shape
    group = shards // CODES
    codes = []
    for g in range(CODES):
        terms = arrived_ref[pl.ds(g * group, group)].astype(jnp.float32)
        total = jnp.sum(terms, axis=1).reshape(group * rows, width)
        peak = jnp.maximum(jnp.max(jnp.abs(total), axis=0, keepdims=True), FLOOR)
        code = jnp.ceil(jnp.log(peak) * STEPS)
        units = jnp.floor(total * (1.0 / scale_of(code)) + 0.5)
        units = jnp.clip(units, -TOP, TOP).astype(jnp.int32).astype(jnp.int16)
        packed_ref[pl.ds(g * group * rows, group * rows), :] = units
        codes.append(code)
    codes = jnp.concatenate(codes, axis=0).astype(jnp.int32).astype(jnp.int16)
    packed_ref[pl.ds(shards * rows, CODES), :] = codes
    packed_ref[pl.ds(shards * rows + CODES, root_ref.shape[0]), :] = root_ref[...]


def fold(arrived, root):
    shards, replicas, rows, width = arrived.shape
    return pl.pallas_call(
        fold_kernel,
        out_shape=jax.ShapeDtypeStruct((shards * rows + CODES + root.shape[0], width), jnp.int16),
        in_specs=[vmem()] * 2,
        out_specs=vmem(),
        compiler_params=pltpu.CompilerParams(vmem_limit_bytes=16 * MIB),
        cost_estimate=cost(arrived.size, 2 * arrived.size),
        name="fold",
    )(arrived, root)


def unpack(spread_ref, k, high, low):
    width = spread_ref.shape[2]
    size = high.shape[0]
    rows = size // CODES
    columns = pl.ds(k * width, width)
    scales = scale_of(spread_ref[k, pl.ds(size, CODES), :].astype(jnp.int32).astype(jnp.float32))
    square = jnp.zeros((8, width), jnp.float32)
    for g in range(CODES):
        here = pl.ds(g * rows, rows)
        units = spread_ref[k, here, :].astype(jnp.int32).astype(jnp.float32)
        values = units * scales[g : g + 1]
        upper = values.astype(jnp.bfloat16)
        high[here, columns] = upper
        low[here, columns] = (values - upper.astype(jnp.float32)).astype(jnp.bfloat16)
        square = square + jnp.sum((values * values).reshape(rows // 8, 8, width), axis=0)
    return square


def decode(spread_ref, i, left):
    slabs, rows, size = spread_ref.shape
    start = left.shape[0] + CODES
    for d in range((rows - start) // size):
        code = spread_ref[i, pl.ds(start + d * size, size), :].astype(jnp.int32)
        count = jnp.abs(code) - 1
        depth = lax.shift_right_arithmetic(count, 7)
        value = ((count & 127) + 128).astype(jnp.float32) * (1.0 / 64.0)
        for bit in BITS:
            value = jnp.where((depth & bit) != 0, value * (2.0**-bit), value)
        value = jnp.where(code < 0, -value, value)
        value = jnp.where(code == 0, 0.0, value)
        j = (i + d) % slabs
        left[pl.ds(i * size, size), pl.ds(j * size, size)] = value.astype(jnp.bfloat16)
        if 0 < d < slabs - d:
            left[pl.ds(j * size, size), pl.ds(i * size, size)] = value.T.astype(jnp.bfloat16)


NT = (((1,), (1,)), ((), ()))
NN = (((1,), (0,)), ((), ()))


def dot(a, b, dims):
    return lax.dot_general(a, b, dims, preferred_element_type=jnp.float32)


def shape_kernel(spread_ref, right_ref, out_ref, squares_ref, total_ref, high, low, mid, left_ref):
    slabs = spread_ref.shape[0]
    size, width = out_ref.shape
    tile = 256
    square = jnp.zeros((8, width), jnp.float32)
    for k in range(slabs):
        square = square + unpack(spread_ref, k, high, low)
        decode(spread_ref, k, left_ref)
    total_ref[...] = square

    def right_step(t, carry):
        rows = pl.ds(pl.multiple_of(t * tile, tile), tile)
        part = dot(high[rows, :], right_ref[...], NT) + dot(low[rows, :], right_ref[...], NT)
        upper = part.astype(jnp.bfloat16)
        mid[rows, pl.ds(0, width)] = upper
        mid[rows, pl.ds(width, width)] = (part - upper.astype(jnp.float32)).astype(jnp.bfloat16)
        return carry

    lax.fori_loop(0, size // tile, right_step, 0)

    def left_step(t, square):
        rows = pl.ds(pl.multiple_of(t * tile, tile), tile)
        both = dot(left_ref[rows, :], mid[...], NN)
        part = both[:, :width] + both[:, width:]
        out_ref[rows, :] = part
        return square + jnp.sum((part * part).reshape(tile // 8, 8, width), axis=0)

    square = lax.fori_loop(0, size // tile, left_step, jnp.zeros((8, width), jnp.float32))
    squares_ref[...] = jnp.broadcast_to(jnp.sum(square, axis=0, keepdims=True), (slabs, width))


def shape(spread, right):
    slabs, _, width = spread.shape
    size = right.shape[1]
    return pl.pallas_call(
        shape_kernel,
        out_shape=(
            jax.ShapeDtypeStruct((size, width), jnp.float32),
            jax.ShapeDtypeStruct((slabs, width), jnp.float32),
            jax.ShapeDtypeStruct((8, width), jnp.float32),
        ),
        in_specs=[vmem()] * 2,
        out_specs=(vmem(),) * 3,
        scratch_shapes=[
            pltpu.VMEM((size, size), jnp.bfloat16),
            pltpu.VMEM((size, size), jnp.bfloat16),
            pltpu.VMEM((size, 2 * width), jnp.bfloat16),
            pltpu.VMEM((size, size), jnp.bfloat16),
        ],
        compiler_params=pltpu.CompilerParams(vmem_limit_bytes=24 * MIB),
        cost_estimate=cost(8 * size * size * width, 6 * size * size),
        name="shape",
    )(spread, right)


def graft_kernel(shaped_ref, squares_ref, total_ref, out_ref):
    def whole(x):
        return jnp.sum(jnp.sum(x, axis=0, keepdims=True), axis=1, keepdims=True)

    shaped_square = whole(squares_ref[...])
    block_square = whole(total_ref[...])
    ratio = jnp.sqrt((block_square + EPSILON) / (shaped_square + EPSILON))
    out_ref[...] = (shaped_ref[...] * ratio).astype(jnp.bfloat16)


def graft(shaped, squares, total):
    return pl.pallas_call(
        graft_kernel,
        out_shape=jax.ShapeDtypeStruct(shaped.shape, jnp.bfloat16),
        in_specs=[vmem()] * 3,
        out_specs=vmem(),
        compiler_params=pltpu.CompilerParams(vmem_limit_bytes=8 * MIB),
        cost_estimate=cost(shaped.size, 6 * shaped.size),
        name="graft",
    )(shaped, squares, total)


def stats_kernel(place_ref, spread_ref, left_ref, right_ref, left_out, right_out, high, low, turned):
    slabs = spread_ref.shape[0]
    rows, size = left_ref.shape
    tile = 256
    for k in range(slabs):
        unpack(spread_ref, k, high, low)
    own = pl.ds(pl.multiple_of(place_ref[0] * rows, rows), rows)
    turned[pl.ds(0, rows), :] = high[:, own].T
    turned[pl.ds(rows, rows), :] = low[:, own].T

    def step(t, carry):
        here = pl.ds(pl.multiple_of(t * tile, tile), tile)
        part = dot(high[own, :], high[here, :], NT)
        part += dot(low[own, :], high[here, :], NT)
        part += dot(high[own, :], low[here, :], NT)
        left_out[:, here] = DECAY_RATE * left_ref[:, here] + (1.0 - DECAY_RATE) * part
        both = dot(turned[...], high[:, here], NN)
        part = both[:rows] + both[rows:] + dot(turned[pl.ds(0, rows), :], low[:, here], NN)
        right_out[:, here] = DECAY_RATE * right_ref[:, here] + (1.0 - DECAY_RATE) * part
        return carry

    lax.fori_loop(0, size // tile, step, 0)


def stats(place, spread, left, right):
    rows, size = left.shape
    return pl.pallas_call(
        stats_kernel,
        out_shape=(jax.ShapeDtypeStruct(left.shape, left.dtype),) * 2,
        in_specs=[pl.BlockSpec(memory_space=pltpu.SMEM)] + [vmem()] * 3,
        out_specs=(vmem(),) * 2,
        scratch_shapes=[
            pltpu.VMEM((size, size), jnp.bfloat16),
            pltpu.VMEM((size, size), jnp.bfloat16),
            pltpu.VMEM((2 * rows, size), jnp.bfloat16),
        ],
        compiler_params=pltpu.CompilerParams(vmem_limit_bytes=24 * MIB),
        cost_estimate=cost(12 * size * size * rows, 6 * size * size),
        name="stats",
    )(place, spread, left, right)


def encode_kernel(place_ref, left_ref, code_ref):
    size = left_ref.shape[0]
    slabs = left_ref.shape[1] // size
    for d in range(code_ref.shape[0] // size):
        column = lax.rem(place_ref[0] + d, slabs) * size
        value = left_ref[:, pl.ds(pl.multiple_of(column, size), size)].astype(jnp.float32)
        rest = jnp.abs(value)
        depth = jnp.zeros(value.shape, jnp.float32)
        for bit in BITS:
            scaled = rest * (2.0**bit)
            keep = scaled < 4.0
            rest = jnp.where(keep, scaled, rest)
            depth = jnp.where(keep, depth + bit, depth)
        code = jnp.where(value == 0.0, 0.0, depth * 128.0 + rest * 64.0 - 127.0)
        code = jnp.where(value < 0.0, -code, code)
        code_ref[pl.ds(d * size, size), :] = code.astype(jnp.int32).astype(jnp.int16)


def encode(place, left, slabs):
    rows = left.shape[0]
    count = slabs // 2 + 1
    return pl.pallas_call(
        encode_kernel,
        out_shape=jax.ShapeDtypeStruct((count * rows, rows), jnp.int16),
        in_specs=[pl.BlockSpec(memory_space=pltpu.SMEM), vmem()],
        out_specs=vmem(),
        compiler_params=pltpu.CompilerParams(vmem_limit_bytes=8 * MIB),
        cost_estimate=cost(30 * count * rows * rows, 4 * left.size),
        name="encode",
    )(place, left)


def body(grads, assign, left_factor, right_factor, left_root, right_root):
    fsdp_size = lax.axis_size("fsdp")
    dp_size = lax.axis_size("dp")
    shard_rows = grads.shape[2]
    width = grads.shape[3]
    col_width = width // dp_size
    place = lax.axis_index("dp").astype(jnp.int32).reshape(1)
    outgoing = send(assign, grads[0], dp_size)
    outgoing = outgoing.reshape(fsdp_size * dp_size, shard_rows, col_width)
    outgoing, left_rows = lax.optimization_barrier((outgoing, left_root[0]))
    codes = encode(place, left_rows, dp_size)
    arrived = lax.all_to_all(outgoing, ("fsdp", "dp"), split_axis=0, concat_axis=0, tiled=True)
    packed = fold(arrived.reshape(fsdp_size, dp_size, shard_rows, col_width), codes)
    spread = lax.all_gather(packed, "dp", axis=0)
    shaped, squares, total = shape(spread, right_root[0])
    squares = lax.all_to_all(squares, "dp", split_axis=0, concat_axis=0, tiled=True)
    rounded = graft(shaped, squares, total).reshape(fsdp_size, shard_rows, col_width)
    rounded, spread = lax.optimization_barrier((rounded, spread))
    returned = lax.all_to_all(rounded, "fsdp", split_axis=0, concat_axis=0, tiled=True)
    left_out, right_out = stats(place, spread, left_factor[0], right_factor[0])
    update = jnp.take(returned, assign, axis=0, mode="clip")
    return (update, left_out[None], right_out[None])


def solution(mesh):
    placed = (
        P("dp", None, "fsdp", None),
        P(),
        P("fsdp", "dp", None),
        P("fsdp", "dp", None),
        P("fsdp", "dp", None),
        P("fsdp", "dp", None),
    )
    return jax.shard_map(
        body,
        mesh=mesh,
        in_specs=placed,
        out_specs=(P(None, "fsdp", "dp"), P("fsdp", "dp", None), P("fsdp", "dp", None)),
        check_vma=False,
    )
```

```python
import functools

import jax
import jax.numpy as jnp
from jax import lax
from jax.experimental import pallas as pl
from jax.experimental.pallas import tpu as pltpu
from jax.sharding import PartitionSpec as P

DECAY_RATE = 0.999
EPSILON = 1e-06
STEPS = 90.0
TOP = 32767.0
FLOOR = 1e-30
CODES = 16
BITS = (64, 32, 16, 8, 4, 2, 1)
MIB = 1 << 20


def vmem():
    return pl.BlockSpec(memory_space=pltpu.VMEM)


def anywhere():
    return pl.BlockSpec(memory_space=pl.ANY)


def cost(flops, moved):
    return pl.CostEstimate(flops=flops, bytes_accessed=moved, transcendentals=0)


def send_kernel(dp_size, assign_ref, grads_ref, out_ref, held, turned, in_sems, out_sem):
    blocks = grads_ref.shape[0]
    col_width = grads_ref.shape[2] // dp_size
    chunks = in_sems.shape[0]
    chunk = blocks // chunks
    loads = [
        pltpu.make_async_copy(
            grads_ref.at[pl.ds(c * chunk, chunk)], held.at[pl.ds(c * chunk, chunk)], in_sems.at[c]
        )
        for c in range(chunks)
    ]
    for load in loads:
        load.start()
    for c in range(chunks):
        loads[c].wait()

        def turn(b, carry):
            for k in range(dp_size):
                turned[b, k] = held[b, :, pl.ds(k * col_width, col_width)]
            pltpu.make_async_copy(turned.at[b], out_ref.at[assign_ref[b]], out_sem).start()
            return carry

        lax.fori_loop(c * chunk, (c + 1) * chunk, turn, 0, unroll=True)
    pltpu.make_async_copy(turned, out_ref, out_sem).wait()


def send(assign, grads, dp_size):
    blocks, rows, width = grads.shape
    shape = (blocks, dp_size, rows, width // dp_size)
    return pl.pallas_call(
        functools.partial(send_kernel, dp_size),
        out_shape=jax.ShapeDtypeStruct(shape, grads.dtype),
        in_specs=[pl.BlockSpec(memory_space=pltpu.SMEM), anywhere()],
        out_specs=anywhere(),
        scratch_shapes=[
            pltpu.VMEM(grads.shape, grads.dtype),
            pltpu.VMEM(shape, grads.dtype),
            pltpu.SemaphoreType.DMA((8,)),
            pltpu.SemaphoreType.DMA,
        ],
        compiler_params=pltpu.CompilerParams(vmem_limit_bytes=60 * MIB),
        cost_estimate=cost(0, 2 * grads.size * 2),
        name="send",
    )(assign, grads)


def scale_of(code):
    return jnp.exp(code * (1.0 / STEPS)) * (1.0 / TOP)


def fold_kernel(arrived_ref, root_ref, packed_ref, square_ref):
    shards, replicas, rows, width = arrived_ref.shape
    group = shards // CODES
    codes = []
    square = jnp.zeros((8, width), jnp.float32)
    for g in range(CODES):
        terms = arrived_ref[pl.ds(g * group, group)].astype(jnp.float32)
        total = jnp.sum(terms, axis=1).reshape(group * rows, width)
        peak = jnp.maximum(jnp.max(jnp.abs(total), axis=0, keepdims=True), FLOOR)
        code = jnp.ceil(jnp.log(peak) * STEPS)
        units = jnp.floor(total * (1.0 / scale_of(code)) + 0.5)
        units = jnp.clip(units, -TOP, TOP).astype(jnp.int32).astype(jnp.int16)
        packed_ref[pl.ds(g * group * rows, group * rows), :] = units
        codes.append(code)
        square = square + jnp.sum((total * total).reshape(group * rows // 8, 8, width), axis=0)
    square_ref[...] = square
    codes = jnp.concatenate(codes, axis=0).astype(jnp.int32).astype(jnp.int16)
    packed_ref[pl.ds(shards * rows, CODES), :] = codes
    packed_ref[pl.ds(shards * rows + CODES, root_ref.shape[0]), :] = root_ref[...]


def fold(arrived, root):
    shards, replicas, rows, width = arrived.shape
    return pl.pallas_call(
        fold_kernel,
        out_shape=(
            jax.ShapeDtypeStruct((shards * rows + CODES + root.shape[0], width), jnp.int16),
            jax.ShapeDtypeStruct((8, width), jnp.float32),
        ),
        in_specs=[vmem()] * 2,
        out_specs=(vmem(),) * 2,
        compiler_params=pltpu.CompilerParams(vmem_limit_bytes=16 * MIB),
        cost_estimate=cost(arrived.size, 2 * arrived.size),
        name="fold",
    )(arrived, root)


def unpack(spread_ref, k, high, low):
    width = spread_ref.shape[2]
    size = high.shape[0]
    rows = size // CODES
    columns = pl.ds(k * width, width)
    scales = scale_of(spread_ref[k, pl.ds(size, CODES), :].astype(jnp.int32).astype(jnp.float32))
    for g in range(CODES):
        here = pl.ds(g * rows, rows)
        units = spread_ref[k, here, :].astype(jnp.int32).astype(jnp.float32)
        values = units * scales[g : g + 1]
        upper = values.astype(jnp.bfloat16)
        high[here, columns] = upper
        low[here, columns] = (values - upper.astype(jnp.float32)).astype(jnp.bfloat16)


def decode(spread_ref, i, left):
    slabs, rows, size = spread_ref.shape
    start = left.shape[0] + CODES
    for d in range((rows - start) // size):
        code = spread_ref[i, pl.ds(start + d * size, size), :].astype(jnp.int32)
        count = jnp.abs(code) - 1
        power = jnp.exp2((1 - lax.shift_right_arithmetic(count, 7)).astype(jnp.float32))
        value = ((count & 127) + 128).astype(jnp.float32) * (1.0 / 128.0) * power
        value = jnp.where(code < 0, -value, value)
        value = jnp.where(code == 0, 0.0, value).astype(jnp.bfloat16)
        j = (i + d) % slabs
        left[pl.ds(i * size, size), pl.ds(j * size, size)] = value
        if 0 < d < slabs - d:
            left[pl.ds(j * size, size), pl.ds(i * size, size)] = value.T


NT = (((1,), (1,)), ((), ()))
NN = (((1,), (0,)), ((), ()))


def dot(a, b, dims):
    return lax.dot_general(a, b, dims, preferred_element_type=jnp.float32)


def halves(a, b):
    a, b = (jnp.sum(x, axis=0, keepdims=True) for x in (a, b))
    width = a.shape[1]
    lane = lax.broadcasted_iota(jnp.int32, a.shape, 1)
    a, b = (x + pltpu.roll(x, width // 2, 1) for x in (a, b))
    return jnp.where(lane < width // 2, a, b)


def shape_kernel(spread_ref, right_ref, square_ref, out_ref, squares_ref, high, low, mid, left_ref):
    slabs = spread_ref.shape[0]
    size, width = out_ref.shape
    tile = 256
    for k in range(slabs):
        unpack(spread_ref, k, high, low)
        decode(spread_ref, k, left_ref)

    def right_step(t, carry):
        rows = pl.ds(pl.multiple_of(t * tile, tile), tile)
        part = dot(high[rows, :], right_ref[...], NT) + dot(low[rows, :], right_ref[...], NT)
        upper = part.astype(jnp.bfloat16)
        mid[rows, pl.ds(0, width)] = upper
        mid[rows, pl.ds(width, width)] = (part - upper.astype(jnp.float32)).astype(jnp.bfloat16)
        return carry

    lax.fori_loop(0, size // tile, right_step, 0)

    square = jnp.zeros((8, width), jnp.float32)
    for t in range(size // tile):
        both = dot(left_ref[pl.ds(t * tile, tile), :], mid[...], NN)
        part = both[:, :width] + both[:, width:]
        square = square + jnp.sum((part * part).reshape(tile // 8, 8, width), axis=0)
        out_ref[pl.ds(t * tile, tile), :] = part
    squares_ref[...] = jnp.broadcast_to(halves(square, square_ref[...]), (slabs, width))


def shape(spread, right, square):
    slabs, _, width = spread.shape
    size = right.shape[1]
    return pl.pallas_call(
        shape_kernel,
        out_shape=(
            jax.ShapeDtypeStruct((size, width), jnp.float32),
            jax.ShapeDtypeStruct((slabs, width), jnp.float32),
        ),
        in_specs=[vmem()] * 3,
        out_specs=(vmem(),) * 2,
        scratch_shapes=[
            pltpu.VMEM((size, size), jnp.bfloat16),
            pltpu.VMEM((size, size), jnp.bfloat16),
            pltpu.VMEM((size, 2 * width), jnp.bfloat16),
            pltpu.VMEM((size, size), jnp.bfloat16),
        ],
        compiler_params=pltpu.CompilerParams(vmem_limit_bytes=24 * MIB),
        cost_estimate=cost(8 * size * size * width, 6 * size * size),
        name="shape",
    )(spread, right, square)


def graft_kernel(squares_ref, shaped_ref, out_ref):
    total = jnp.sum(squares_ref[...], axis=0, keepdims=True)
    first = lax.broadcasted_iota(jnp.int32, total.shape, 1) < total.shape[1] // 2
    shaped_square = jnp.sum(jnp.where(first, total, 0.0), axis=1, keepdims=True)
    block_square = jnp.sum(jnp.where(first, 0.0, total), axis=1, keepdims=True)
    ratio = jnp.sqrt((block_square + EPSILON) / (shaped_square + EPSILON))
    out_ref[...] = (shaped_ref[...] * ratio).astype(jnp.bfloat16)


def graft(squares, shaped):
    return pl.pallas_call(
        graft_kernel,
        out_shape=jax.ShapeDtypeStruct(shaped.shape, jnp.bfloat16),
        in_specs=[vmem()] * 2,
        out_specs=vmem(),
        compiler_params=pltpu.CompilerParams(vmem_limit_bytes=8 * MIB),
        cost_estimate=cost(shaped.size, 6 * shaped.size),
        name="graft",
    )(squares, shaped)


def place_kernel(assign_ref, returned_ref, out_ref):
    for b in range(out_ref.shape[0]):
        out_ref[b] = returned_ref[assign_ref[b]]


def place_blocks(assign, returned):
    return pl.pallas_call(
        place_kernel,
        out_shape=jax.ShapeDtypeStruct(returned.shape, returned.dtype),
        in_specs=[pl.BlockSpec(memory_space=pltpu.SMEM), vmem()],
        out_specs=vmem(),
        compiler_params=pltpu.CompilerParams(vmem_limit_bytes=8 * MIB),
        cost_estimate=cost(0, 4 * returned.size),
        name="place",
    )(assign, returned)


def stats_kernel(place_ref, spread_ref, left_ref, right_ref, left_out, right_out, high, low, turned):
    slabs = spread_ref.shape[0]
    rows, size = left_ref.shape
    tile = 256
    for k in range(slabs):
        unpack(spread_ref, k, high, low)
    own = pl.ds(pl.multiple_of(place_ref[0] * rows, rows), rows)
    turned[pl.ds(0, rows), :] = high[:, own].T
    turned[pl.ds(rows, rows), :] = low[:, own].T

    def step(t, carry):
        here = pl.ds(pl.multiple_of(t * tile, tile), tile)
        part = dot(high[own, :], high[here, :], NT)
        part += dot(low[own, :], high[here, :], NT)
        part += dot(high[own, :], low[here, :], NT)
        left_out[:, here] = DECAY_RATE * left_ref[:, here] + (1.0 - DECAY_RATE) * part
        both = dot(turned[...], high[:, here], NN)
        part = both[:rows] + both[rows:] + dot(turned[pl.ds(0, rows), :], low[:, here], NN)
        right_out[:, here] = DECAY_RATE * right_ref[:, here] + (1.0 - DECAY_RATE) * part
        return carry

    lax.fori_loop(0, size // tile, step, 0)


def stats(place, spread, left, right):
    rows, size = left.shape
    return pl.pallas_call(
        stats_kernel,
        out_shape=(jax.ShapeDtypeStruct(left.shape, left.dtype),) * 2,
        in_specs=[pl.BlockSpec(memory_space=pltpu.SMEM)] + [vmem()] * 3,
        out_specs=(vmem(),) * 2,
        scratch_shapes=[
            pltpu.VMEM((size, size), jnp.bfloat16),
            pltpu.VMEM((size, size), jnp.bfloat16),
            pltpu.VMEM((2 * rows, size), jnp.bfloat16),
        ],
        compiler_params=pltpu.CompilerParams(vmem_limit_bytes=24 * MIB),
        cost_estimate=cost(12 * size * size * rows, 6 * size * size),
        name="stats",
    )(place, spread, left, right)


def encode_kernel(place_ref, left_ref, code_ref):
    size = left_ref.shape[0]
    slabs = left_ref.shape[1] // size
    for d in range(code_ref.shape[0] // size):
        column = lax.rem(place_ref[0] + d, slabs) * size
        value = left_ref[:, pl.ds(pl.multiple_of(column, size), size)].astype(jnp.float32)
        rest = jnp.abs(value)
        depth = jnp.zeros(value.shape, jnp.float32)
        for bit in BITS:
            scaled = rest * (2.0**bit)
            keep = scaled < 4.0
            rest = jnp.where(keep, scaled, rest)
            depth = jnp.where(keep, depth + bit, depth)
        code = jnp.where(value == 0.0, 0.0, depth * 128.0 + rest * 64.0 - 127.0)
        code = jnp.where(value < 0.0, -code, code)
        code_ref[pl.ds(d * size, size), :] = code.astype(jnp.int32).astype(jnp.int16)


def encode(place, left, slabs):
    rows = left.shape[0]
    count = slabs // 2 + 1
    return pl.pallas_call(
        encode_kernel,
        out_shape=jax.ShapeDtypeStruct((count * rows, rows), jnp.int16),
        in_specs=[pl.BlockSpec(memory_space=pltpu.SMEM), vmem()],
        out_specs=vmem(),
        compiler_params=pltpu.CompilerParams(vmem_limit_bytes=8 * MIB),
        cost_estimate=cost(30 * count * rows * rows, 4 * left.size),
        name="encode",
    )(place, left)


def body(grads, assign, left_factor, right_factor, left_root, right_root):
    fsdp_size = lax.axis_size("fsdp")
    dp_size = lax.axis_size("dp")
    shard_rows = grads.shape[2]
    width = grads.shape[3]
    col_width = width // dp_size
    place = lax.axis_index("dp").astype(jnp.int32).reshape(1)
    outgoing = send(assign, grads[0], dp_size)
    outgoing = outgoing.reshape(fsdp_size * dp_size, shard_rows, col_width)
    outgoing, left_rows = lax.optimization_barrier((outgoing, left_root[0]))
    codes = encode(place, left_rows, dp_size)
    arrived = lax.all_to_all(outgoing, ("fsdp", "dp"), split_axis=0, concat_axis=0, tiled=True)
    packed, square = fold(arrived.reshape(fsdp_size, dp_size, shard_rows, col_width), codes)
    spread = lax.all_gather(packed, "dp", axis=0)
    shaped, squares = shape(spread, right_root[0], square)
    squares = lax.all_to_all(squares, "dp", split_axis=0, concat_axis=0, tiled=True)
    rounded = graft(squares, shaped).reshape(fsdp_size, shard_rows, col_width)
    rounded, spread = lax.optimization_barrier((rounded, spread))
    returned = lax.all_to_all(rounded, "fsdp", split_axis=0, concat_axis=0, tiled=True)
    left_out, right_out = stats(place, spread, left_factor[0], right_factor[0])
    update = place_blocks(assign, returned)
    return (update, left_out[None], right_out[None])


def solution(mesh):
    placed = (
        P("dp", None, "fsdp", None),
        P(),
        P("fsdp", "dp", None),
        P("fsdp", "dp", None),
        P("fsdp", "dp", None),
        P("fsdp", "dp", None),
    )
    return jax.shard_map(
        body,
        mesh=mesh,
        in_specs=placed,
        out_specs=(P(None, "fsdp", "dp"), P("fsdp", "dp", None), P("fsdp", "dp", None)),
        check_vma=False,
    )
```

```python
import functools

import jax
import jax.numpy as jnp
from jax import lax
from jax.experimental import pallas as pl
from jax.experimental.pallas import tpu as pltpu
from jax.sharding import PartitionSpec as P

DECAY_RATE = 0.999
EPSILON = 1e-06
STEPS = 90.0
TOP = 32767.0
FLOOR = 1e-30
CODES = 16
BITS = (64, 32, 16, 8, 4, 2, 1)
MIB = 1 << 20


def vmem():
    return pl.BlockSpec(memory_space=pltpu.VMEM)


def anywhere():
    return pl.BlockSpec(memory_space=pl.ANY)


def cost(flops, moved):
    return pl.CostEstimate(flops=flops, bytes_accessed=moved, transcendentals=0)


def send_kernel(dp_size, assign_ref, grads_ref, out_ref, held, turned, in_sems, out_sem):
    blocks = grads_ref.shape[0]
    col_width = grads_ref.shape[2] // dp_size
    chunks = in_sems.shape[0]
    chunk = blocks // chunks
    loads = [
        pltpu.make_async_copy(
            grads_ref.at[pl.ds(c * chunk, chunk)], held.at[pl.ds(c * chunk, chunk)], in_sems.at[c]
        )
        for c in range(chunks)
    ]
    for load in loads:
        load.start()
    for c in range(chunks):
        loads[c].wait()

        def turn(b, carry):
            for k in range(dp_size):
                turned[b, k] = held[b, :, pl.ds(k * col_width, col_width)]
            pltpu.make_async_copy(turned.at[b], out_ref.at[assign_ref[b]], out_sem).start()
            return carry

        lax.fori_loop(c * chunk, (c + 1) * chunk, turn, 0, unroll=True)
    pltpu.make_async_copy(turned, out_ref, out_sem).wait()


def send(assign, grads, dp_size):
    blocks, rows, width = grads.shape
    shape = (blocks, dp_size, rows, width // dp_size)
    return pl.pallas_call(
        functools.partial(send_kernel, dp_size),
        out_shape=jax.ShapeDtypeStruct(shape, grads.dtype),
        in_specs=[pl.BlockSpec(memory_space=pltpu.SMEM), anywhere()],
        out_specs=anywhere(),
        scratch_shapes=[
            pltpu.VMEM(grads.shape, grads.dtype),
            pltpu.VMEM(shape, grads.dtype),
            pltpu.SemaphoreType.DMA((8,)),
            pltpu.SemaphoreType.DMA,
        ],
        compiler_params=pltpu.CompilerParams(vmem_limit_bytes=60 * MIB),
        cost_estimate=cost(0, 2 * grads.size * 2),
        name="send",
    )(assign, grads)


def scale_of(code):
    return jnp.exp(code * (1.0 / STEPS)) * (1.0 / TOP)


def fold_kernel(arrived_ref, root_ref, packed_ref, square_ref):
    shards, replicas, rows, width = arrived_ref.shape
    group = shards // CODES
    codes = []
    square = jnp.zeros((8, width), jnp.float32)
    for g in range(CODES):
        terms = arrived_ref[pl.ds(g * group, group)].astype(jnp.float32)
        total = jnp.sum(terms, axis=1).reshape(group * rows, width)
        peak = jnp.maximum(jnp.max(jnp.abs(total), axis=0, keepdims=True), FLOOR)
        code = jnp.ceil(jnp.log(peak) * STEPS)
        units = jnp.floor(total * (1.0 / scale_of(code)) + 0.5)
        units = jnp.clip(units, -TOP, TOP).astype(jnp.int32).astype(jnp.int16)
        packed_ref[pl.ds(g * group * rows, group * rows), :] = units
        codes.append(code)
        square = square + jnp.sum((total * total).reshape(group * rows // 8, 8, width), axis=0)
    square_ref[...] = square
    codes = jnp.concatenate(codes, axis=0).astype(jnp.int32).astype(jnp.int16)
    packed_ref[pl.ds(shards * rows, CODES), :] = codes
    packed_ref[pl.ds(shards * rows + CODES, root_ref.shape[0]), :] = root_ref[...]


def fold(arrived, root):
    shards, replicas, rows, width = arrived.shape
    return pl.pallas_call(
        fold_kernel,
        out_shape=(
            jax.ShapeDtypeStruct((shards * rows + CODES + root.shape[0], width), jnp.int16),
            jax.ShapeDtypeStruct((8, width), jnp.float32),
        ),
        in_specs=[vmem()] * 2,
        out_specs=(vmem(),) * 2,
        compiler_params=pltpu.CompilerParams(vmem_limit_bytes=16 * MIB),
        cost_estimate=cost(arrived.size, 2 * arrived.size),
        name="fold",
    )(arrived, root)


def unpack(spread_ref, k, high, low, first, count):
    width = spread_ref.shape[2]
    size = high.shape[0]
    rows = size // CODES
    columns = pl.ds(k * width, width)
    scales = scale_of(spread_ref[k, pl.ds(size, CODES), :].astype(jnp.int32).astype(jnp.float32))
    for g in range(first // rows, (first + count) // rows):
        here = pl.ds(g * rows, rows)
        units = spread_ref[k, here, :].astype(jnp.int32).astype(jnp.float32)
        values = units * scales[g : g + 1]
        upper = values.astype(jnp.bfloat16)
        high[here, columns] = upper
        low[here, columns] = (values - upper.astype(jnp.float32)).astype(jnp.bfloat16)


def values_of(code):
    code = code.astype(jnp.int32)
    count = jnp.abs(code) - 1
    power = jnp.exp2((1 - lax.shift_right_arithmetic(count, 7)).astype(jnp.float32))
    value = ((count & 127) + 128).astype(jnp.float32) * (1.0 / 128.0) * power
    value = jnp.where(code < 0, -value, value)
    return jnp.where(code == 0, 0.0, value).astype(jnp.bfloat16)


def decode(spread_ref, i, left):
    slabs, _, size = spread_ref.shape
    half = slabs // 2
    start = left.shape[0] + CODES

    def at(a, b):
        return pl.ds(a * size, size), pl.ds(b * size, size)

    for d in range(half):
        value = values_of(spread_ref[i, pl.ds(start + d * size, size), :])
        j = (i + d) % slabs
        left[at(i, j)] = value
        if d:
            left[at(j, i)] = value.T
    if i < half:
        rest = pl.ds(start + half * size, size // 2)
        value = values_of(jnp.concatenate([spread_ref[i, rest, :], spread_ref[i + half, rest, :]], axis=0))
        left[at(i, i + half)] = value
        left[at(i + half, i)] = value.T


NT = (((1,), (1,)), ((), ()))
NN = (((1,), (0,)), ((), ()))


def dot(a, b, dims):
    return lax.dot_general(a, b, dims, preferred_element_type=jnp.float32)


def halves(a, b):
    a, b = (jnp.sum(x, axis=0, keepdims=True) for x in (a, b))
    width = a.shape[1]
    lane = lax.broadcasted_iota(jnp.int32, a.shape, 1)
    a, b = (x + pltpu.roll(x, width // 2, 1) for x in (a, b))
    return jnp.where(lane < width // 2, a, b)


def shape_kernel(spread_ref, right_ref, square_ref, out_ref, squares_ref, high, low, mid, left_ref):
    slabs = spread_ref.shape[0]
    size, width = out_ref.shape
    tile = 256
    for t in range(size // tile):
        rows = pl.ds(t * tile, tile)
        for k in range(slabs):
            unpack(spread_ref, k, high, low, t * tile, tile)
        decode(spread_ref, 2 * t, left_ref)
        decode(spread_ref, 2 * t + 1, left_ref)
        part = dot(high[rows, :], right_ref[...], NT) + dot(low[rows, :], right_ref[...], NT)
        upper = part.astype(jnp.bfloat16)
        mid[rows, pl.ds(0, width)] = upper
        mid[rows, pl.ds(width, width)] = (part - upper.astype(jnp.float32)).astype(jnp.bfloat16)

    square = jnp.zeros((8, width), jnp.float32)
    for t in range(size // tile):
        both = dot(left_ref[pl.ds(t * tile, tile), :], mid[...], NN)
        part = both[:, :width] + both[:, width:]
        square = square + jnp.sum((part * part).reshape(tile // 8, 8, width), axis=0)
        out_ref[pl.ds(t * tile, tile), :] = part
    squares_ref[...] = jnp.broadcast_to(halves(square, square_ref[...]), (slabs, width))


def shape(spread, right, square):
    slabs, _, width = spread.shape
    size = right.shape[1]
    return pl.pallas_call(
        shape_kernel,
        out_shape=(
            jax.ShapeDtypeStruct((size, width), jnp.float32),
            jax.ShapeDtypeStruct((slabs, width), jnp.float32),
        ),
        in_specs=[vmem()] * 3,
        out_specs=(vmem(),) * 2,
        scratch_shapes=[
            pltpu.VMEM((size, size), jnp.bfloat16),
            pltpu.VMEM((size, size), jnp.bfloat16),
            pltpu.VMEM((size, 2 * width), jnp.bfloat16),
            pltpu.VMEM((size, size), jnp.bfloat16),
        ],
        compiler_params=pltpu.CompilerParams(vmem_limit_bytes=24 * MIB),
        cost_estimate=cost(8 * size * size * width, 6 * size * size),
        name="shape",
    )(spread, right, square)


def graft_kernel(squares_ref, shaped_ref, out_ref):
    total = jnp.sum(squares_ref[...], axis=0, keepdims=True)
    first = lax.broadcasted_iota(jnp.int32, total.shape, 1) < total.shape[1] // 2
    shaped_square = jnp.sum(jnp.where(first, total, 0.0), axis=1, keepdims=True)
    block_square = jnp.sum(jnp.where(first, 0.0, total), axis=1, keepdims=True)
    ratio = jnp.sqrt((block_square + EPSILON) / (shaped_square + EPSILON))
    out_ref[...] = (shaped_ref[...] * ratio).astype(jnp.bfloat16)


def graft(squares, shaped):
    return pl.pallas_call(
        graft_kernel,
        out_shape=jax.ShapeDtypeStruct(shaped.shape, jnp.bfloat16),
        in_specs=[vmem()] * 2,
        out_specs=vmem(),
        compiler_params=pltpu.CompilerParams(vmem_limit_bytes=8 * MIB),
        cost_estimate=cost(shaped.size, 6 * shaped.size),
        name="graft",
    )(squares, shaped)


def place_kernel(assign_ref, returned_ref, out_ref):
    for b in range(out_ref.shape[0]):
        out_ref[b] = returned_ref[assign_ref[b]]


def place_blocks(assign, returned):
    return pl.pallas_call(
        place_kernel,
        out_shape=jax.ShapeDtypeStruct(returned.shape, returned.dtype),
        in_specs=[pl.BlockSpec(memory_space=pltpu.SMEM), vmem()],
        out_specs=vmem(),
        compiler_params=pltpu.CompilerParams(vmem_limit_bytes=8 * MIB),
        cost_estimate=cost(0, 4 * returned.size),
        name="place",
    )(assign, returned)


def stats_kernel(place_ref, spread_ref, left_ref, right_ref, left_out, right_out, high, low, turned):
    slabs = spread_ref.shape[0]
    rows, size = left_ref.shape
    tile = 256
    for k in range(slabs):
        unpack(spread_ref, k, high, low, 0, size)
    own = pl.ds(pl.multiple_of(place_ref[0] * rows, rows), rows)
    turned[pl.ds(0, rows), :] = high[:, own].T
    turned[pl.ds(rows, rows), :] = low[:, own].T

    def step(t, carry):
        here = pl.ds(pl.multiple_of(t * tile, tile), tile)
        part = dot(high[own, :], high[here, :], NT)
        part += dot(low[own, :], high[here, :], NT)
        part += dot(high[own, :], low[here, :], NT)
        left_out[:, here] = DECAY_RATE * left_ref[:, here] + (1.0 - DECAY_RATE) * part
        both = dot(turned[...], high[:, here], NN)
        part = both[:rows] + both[rows:] + dot(turned[pl.ds(0, rows), :], low[:, here], NN)
        right_out[:, here] = DECAY_RATE * right_ref[:, here] + (1.0 - DECAY_RATE) * part
        return carry

    lax.fori_loop(0, size // tile, step, 0)


def stats(place, spread, left, right):
    rows, size = left.shape
    return pl.pallas_call(
        stats_kernel,
        out_shape=(jax.ShapeDtypeStruct(left.shape, left.dtype),) * 2,
        in_specs=[pl.BlockSpec(memory_space=pltpu.SMEM)] + [vmem()] * 3,
        out_specs=(vmem(),) * 2,
        scratch_shapes=[
            pltpu.VMEM((size, size), jnp.bfloat16),
            pltpu.VMEM((size, size), jnp.bfloat16),
            pltpu.VMEM((2 * rows, size), jnp.bfloat16),
        ],
        compiler_params=pltpu.CompilerParams(vmem_limit_bytes=24 * MIB),
        cost_estimate=cost(12 * size * size * rows, 6 * size * size),
        name="stats",
    )(place, spread, left, right)


def codes_of(value):
    rest = jnp.abs(value)
    depth = jnp.zeros(value.shape, jnp.float32)
    for bit in BITS:
        scaled = rest * (2.0**bit)
        keep = scaled < 4.0
        rest = jnp.where(keep, scaled, rest)
        depth = jnp.where(keep, depth + bit, depth)
    code = jnp.where(value == 0.0, 0.0, depth * 128.0 + rest * 64.0 - 127.0)
    return jnp.where(value < 0.0, -code, code).astype(jnp.int32).astype(jnp.int16)


def encode_kernel(place_ref, left_ref, code_ref):
    size = left_ref.shape[0]
    slabs = left_ref.shape[1] // size
    half = slabs // 2

    def block(d):
        column = lax.rem(place_ref[0] + d, slabs) * size
        return left_ref[:, pl.ds(pl.multiple_of(column, size), size)].astype(jnp.float32)

    for d in range(half):
        code_ref[pl.ds(d * size, size), :] = codes_of(block(d))
    last = block(half)
    last = jnp.where(place_ref[0] < half, last[: size // 2], last.T[size // 2 :])
    code_ref[pl.ds(half * size, size // 2), :] = codes_of(last)


def encode(place, left, slabs):
    rows = left.shape[0]
    count = slabs * rows // 2 + rows // 2
    return pl.pallas_call(
        encode_kernel,
        out_shape=jax.ShapeDtypeStruct((count, rows), jnp.int16),
        in_specs=[pl.BlockSpec(memory_space=pltpu.SMEM), vmem()],
        out_specs=vmem(),
        compiler_params=pltpu.CompilerParams(vmem_limit_bytes=8 * MIB),
        cost_estimate=cost(30 * count * rows, 4 * left.size),
        name="encode",
    )(place, left)


def body(grads, assign, left_factor, right_factor, left_root, right_root):
    fsdp_size = lax.axis_size("fsdp")
    dp_size = lax.axis_size("dp")
    shard_rows = grads.shape[2]
    width = grads.shape[3]
    col_width = width // dp_size
    place = lax.axis_index("dp").astype(jnp.int32).reshape(1)
    outgoing = send(assign, grads[0], dp_size)
    outgoing = outgoing.reshape(fsdp_size * dp_size, shard_rows, col_width)
    outgoing, left_rows = lax.optimization_barrier((outgoing, left_root[0]))
    codes = encode(place, left_rows, dp_size)
    arrived = lax.all_to_all(outgoing, ("fsdp", "dp"), split_axis=0, concat_axis=0, tiled=True)
    packed, square = fold(arrived.reshape(fsdp_size, dp_size, shard_rows, col_width), codes)
    spread = lax.all_gather(packed, "dp", axis=0)
    shaped, squares = shape(spread, right_root[0], square)
    squares = lax.all_to_all(squares, "dp", split_axis=0, concat_axis=0, tiled=True)
    rounded = graft(squares, shaped).reshape(fsdp_size, shard_rows, col_width)
    rounded, spread = lax.optimization_barrier((rounded, spread))
    returned = lax.all_to_all(rounded, "fsdp", split_axis=0, concat_axis=0, tiled=True)
    left_out, right_out = stats(place, spread, left_factor[0], right_factor[0])
    update = place_blocks(assign, returned)
    return (update, left_out[None], right_out[None])


def solution(mesh):
    placed = (
        P("dp", None, "fsdp", None),
        P(),
        P("fsdp", "dp", None),
        P("fsdp", "dp", None),
        P("fsdp", "dp", None),
        P("fsdp", "dp", None),
    )
    return jax.shard_map(
        body,
        mesh=mesh,
        in_specs=placed,
        out_specs=(P(None, "fsdp", "dp"), P("fsdp", "dp", None), P("fsdp", "dp", None)),
        check_vma=False,
    )
```

```python
import functools

import jax
import jax.numpy as jnp
from jax import lax
from jax.experimental import pallas as pl
from jax.experimental.pallas import tpu as pltpu
from jax.sharding import PartitionSpec as P

DECAY_RATE = 0.999
EPSILON = 1e-06
STEPS = 90.0
TOP = 32767.0
FLOOR = 1e-30
CODES = 8
HEAD = 16
BITS = (64, 32, 16, 8, 4, 2, 1)
MIB = 1 << 20


def vmem():
    return pl.BlockSpec(memory_space=pltpu.VMEM)


def anywhere():
    return pl.BlockSpec(memory_space=pl.ANY)


def cost(flops, moved):
    return pl.CostEstimate(flops=flops, bytes_accessed=moved, transcendentals=0)


def send_kernel(dp_size, assign_ref, grads_ref, out_ref, owner_of, held, turned, assign_sem, in_sems, out_sem):
    blocks = grads_ref.shape[0]
    col_width = grads_ref.shape[2] // dp_size
    chunks = in_sems.shape[0]
    chunk = blocks // chunks
    loads = [
        pltpu.make_async_copy(
            grads_ref.at[pl.ds(c * chunk, chunk)], held.at[pl.ds(c * chunk, chunk)], in_sems.at[c]
        )
        for c in range(chunks)
    ]
    owners = pltpu.make_async_copy(assign_ref, owner_of, assign_sem)
    owners.start()
    for load in loads:
        load.start()
    owners.wait()
    for c in range(chunks):
        loads[c].wait()
        for b in range(c * chunk, (c + 1) * chunk):
            for k in range(dp_size):
                turned[b, k] = held[b, :, pl.ds(k * col_width, col_width)]
            pltpu.make_async_copy(turned.at[b], out_ref.at[owner_of[b]], out_sem).start()
    pltpu.make_async_copy(turned, out_ref, out_sem).wait()


def send(assign, grads, dp_size):
    blocks, rows, width = grads.shape
    shape = (blocks, dp_size, rows, width // dp_size)
    return pl.pallas_call(
        functools.partial(send_kernel, dp_size),
        out_shape=jax.ShapeDtypeStruct(shape, grads.dtype),
        in_specs=[anywhere()] * 2,
        out_specs=anywhere(),
        scratch_shapes=[
            pltpu.SMEM((blocks,), jnp.int32),
            pltpu.VMEM(grads.shape, grads.dtype),
            pltpu.VMEM(shape, grads.dtype),
            pltpu.SemaphoreType.DMA,
            pltpu.SemaphoreType.DMA((8,)),
            pltpu.SemaphoreType.DMA,
        ],
        compiler_params=pltpu.CompilerParams(vmem_limit_bytes=60 * MIB),
        cost_estimate=cost(0, 2 * grads.size * 2),
        name="send",
    )(assign, grads)


def scale_of(code):
    return jnp.exp(code * (1.0 / STEPS)) * (1.0 / TOP)


def fold_kernel(arrived_ref, root_ref, packed_ref, square_ref):
    shards, replicas, rows, width = arrived_ref.shape
    group = shards // CODES
    codes = []
    square = jnp.zeros((8, width), jnp.float32)
    for g in range(CODES):
        terms = arrived_ref[pl.ds(g * group, group)].astype(jnp.float32)
        total = jnp.sum(terms, axis=1).reshape(group * rows, width)
        peak = jnp.maximum(jnp.max(jnp.abs(total), axis=0, keepdims=True), FLOOR)
        code = jnp.ceil(jnp.log(peak) * STEPS)
        units = jnp.floor(total * (1.0 / scale_of(code)) + 0.5)
        units = jnp.clip(units, -TOP, TOP).astype(jnp.int32).astype(jnp.int16)
        packed_ref[pl.ds(g * group * rows, group * rows), :] = units
        codes.append(code)
        square = square + jnp.sum((total * total).reshape(group * rows // 8, 8, width), axis=0)
    square_ref[...] = square
    codes = [code.astype(jnp.int32) for code in codes] + [root_ref[pl.ds(0, HEAD), :].astype(jnp.int32)[CODES:]]
    size = shards * rows
    packed_ref[pl.ds(size, HEAD), :] = jnp.concatenate(codes, axis=0).astype(jnp.int16)
    rest = root_ref.shape[0] - HEAD
    packed_ref[pl.ds(size + HEAD, rest), :] = root_ref[pl.ds(HEAD, rest), :]


def fold(arrived, root):
    shards, replicas, rows, width = arrived.shape
    return pl.pallas_call(
        fold_kernel,
        out_shape=(
            jax.ShapeDtypeStruct((shards * rows + root.shape[0], width), jnp.int16),
            jax.ShapeDtypeStruct((8, width), jnp.float32),
        ),
        in_specs=[vmem()] * 2,
        out_specs=(vmem(),) * 2,
        compiler_params=pltpu.CompilerParams(vmem_limit_bytes=16 * MIB),
        cost_estimate=cost(arrived.size, 2 * arrived.size),
        name="fold",
    )(arrived, root)


def unpack(spread_ref, k, high, low, first, count):
    width = spread_ref.shape[2]
    size = high.shape[0]
    rows = size // CODES
    columns = pl.ds(k * width, width)
    scales = scale_of(spread_ref[k, pl.ds(size, HEAD), :].astype(jnp.int32)[:CODES].astype(jnp.float32))
    for g in range(first // rows, (first + count) // rows):
        here = pl.ds(g * rows, rows)
        units = spread_ref[k, here, :].astype(jnp.int32).astype(jnp.float32)
        values = units * scales[g : g + 1]
        upper = values.astype(jnp.bfloat16)
        high[here, columns] = upper
        low[here, columns] = (values - upper.astype(jnp.float32)).astype(jnp.bfloat16)


def values_of(code):
    code = code.astype(jnp.int32)
    count = jnp.abs(code) - 1
    power = jnp.exp2((1 - lax.shift_right_arithmetic(count, 7)).astype(jnp.float32))
    value = ((count & 127) + 128).astype(jnp.float32) * (1.0 / 128.0) * power
    value = jnp.where(code < 0, -value, value)
    return jnp.where(code == 0, 0.0, value)


def decode(spread_ref, i, left):
    slabs, _, size = spread_ref.shape
    half = slabs // 2
    middle = size // 2
    head = left.shape[0]
    start = head + HEAD

    def at(a, b):
        return pl.ds(a * size, size), pl.ds(b * size, size)

    part = values_of(spread_ref[i, pl.ds(start, middle), :])
    corner = values_of(spread_ref[i, pl.ds(head, HEAD), :].astype(jnp.int32)[CODES : CODES + 1])
    both = jnp.concatenate([part, pltpu.roll(part, middle, 1)], axis=0)
    row = lax.broadcasted_iota(jnp.int32, both.shape, 0)
    lane = lax.broadcasted_iota(jnp.int32, both.shape, 1)
    direct = ((row < middle) & (row <= lane)) | ((row >= middle) & (lane >= middle) & (row > lane))
    value = jnp.where(direct, both, both.T)
    value = jnp.where((row == lane) & (row >= middle), pltpu.roll(corner, middle, 1), value)
    left[at(i, i)] = value.astype(jnp.bfloat16)
    start += middle
    for d in range(1, half):
        value = values_of(spread_ref[i, pl.ds(start, size), :]).astype(jnp.bfloat16)
        j = (i + d) % slabs
        left[at(i, j)] = value
        left[at(j, i)] = value.T
        start += size
    if i < half:
        rest = pl.ds(start, middle)
        value = values_of(jnp.concatenate([spread_ref[i, rest, :], spread_ref[i + half, rest, :]], axis=0))
        value = value.astype(jnp.bfloat16)
        left[at(i, i + half)] = value
        left[at(i + half, i)] = value.T


NT = (((1,), (1,)), ((), ()))
NN = (((1,), (0,)), ((), ()))


def dot(a, b, dims):
    return lax.dot_general(a, b, dims, preferred_element_type=jnp.float32)


def halves(a, b):
    a, b = (jnp.sum(x, axis=0, keepdims=True) for x in (a, b))
    width = a.shape[1]
    lane = lax.broadcasted_iota(jnp.int32, a.shape, 1)
    a, b = (x + pltpu.roll(x, width // 2, 1) for x in (a, b))
    return jnp.where(lane < width // 2, a, b)


def shape_kernel(spread_ref, right_ref, square_ref, out_ref, squares_ref, high, low, mid, left_ref):
    slabs = spread_ref.shape[0]
    size, width = out_ref.shape
    tile = 256
    for t in range(size // tile):
        rows = pl.ds(t * tile, tile)
        for k in range(slabs):
            unpack(spread_ref, k, high, low, t * tile, tile)
        decode(spread_ref, 2 * t, left_ref)
        decode(spread_ref, 2 * t + 1, left_ref)
        part = dot(high[rows, :], right_ref[...], NT) + dot(low[rows, :], right_ref[...], NT)
        upper = part.astype(jnp.bfloat16)
        mid[rows, pl.ds(0, width)] = upper
        mid[rows, pl.ds(width, width)] = (part - upper.astype(jnp.float32)).astype(jnp.bfloat16)

    square = jnp.zeros((8, width), jnp.float32)
    for t in range(size // tile):
        both = dot(left_ref[pl.ds(t * tile, tile), :], mid[...], NN)
        part = both[:, :width] + both[:, width:]
        square = square + jnp.sum((part * part).reshape(tile // 8, 8, width), axis=0)
        out_ref[pl.ds(t * tile, tile), :] = part
    squares_ref[...] = jnp.broadcast_to(halves(square, square_ref[...]), (slabs, width))


def shape(spread, right, square):
    slabs, _, width = spread.shape
    size = right.shape[1]
    return pl.pallas_call(
        shape_kernel,
        out_shape=(
            jax.ShapeDtypeStruct((size, width), jnp.float32),
            jax.ShapeDtypeStruct((slabs, width), jnp.float32),
        ),
        in_specs=[vmem()] * 3,
        out_specs=(vmem(),) * 2,
        scratch_shapes=[
            pltpu.VMEM((size, size), jnp.bfloat16),
            pltpu.VMEM((size, size), jnp.bfloat16),
            pltpu.VMEM((size, 2 * width), jnp.bfloat16),
            pltpu.VMEM((size, size), jnp.bfloat16),
        ],
        compiler_params=pltpu.CompilerParams(vmem_limit_bytes=24 * MIB),
        cost_estimate=cost(8 * size * size * width, 6 * size * size),
        name="shape",
    )(spread, right, square)


def graft_kernel(squares_ref, shaped_ref, out_ref):
    total = jnp.sum(squares_ref[...], axis=0, keepdims=True)
    first = lax.broadcasted_iota(jnp.int32, total.shape, 1) < total.shape[1] // 2
    shaped_square = jnp.sum(jnp.where(first, total, 0.0), axis=1, keepdims=True)
    block_square = jnp.sum(jnp.where(first, 0.0, total), axis=1, keepdims=True)
    ratio = jnp.sqrt((block_square + EPSILON) / (shaped_square + EPSILON))
    out_ref[...] = (shaped_ref[...] * ratio).astype(jnp.bfloat16)


def graft(squares, shaped):
    return pl.pallas_call(
        graft_kernel,
        out_shape=jax.ShapeDtypeStruct(shaped.shape, jnp.bfloat16),
        in_specs=[vmem()] * 2,
        out_specs=vmem(),
        compiler_params=pltpu.CompilerParams(vmem_limit_bytes=8 * MIB),
        cost_estimate=cost(shaped.size, 6 * shaped.size),
        name="graft",
    )(squares, shaped)


def place_kernel(assign_ref, returned_ref, out_ref):
    for b in range(out_ref.shape[0]):
        out_ref[b] = returned_ref[assign_ref[b]]


def place_blocks(assign, returned):
    return pl.pallas_call(
        place_kernel,
        out_shape=jax.ShapeDtypeStruct(returned.shape, returned.dtype),
        in_specs=[pl.BlockSpec(memory_space=pltpu.SMEM), vmem()],
        out_specs=vmem(),
        compiler_params=pltpu.CompilerParams(vmem_limit_bytes=8 * MIB),
        cost_estimate=cost(0, 4 * returned.size),
        name="place",
    )(assign, returned)


def stats_kernel(place_ref, spread_ref, left_ref, right_ref, left_out, right_out, high, low, turned):
    slabs = spread_ref.shape[0]
    rows, size = left_ref.shape
    tile = 256
    for k in range(slabs):
        unpack(spread_ref, k, high, low, 0, size)
    own = pl.ds(pl.multiple_of(place_ref[0] * rows, rows), rows)
    turned[pl.ds(0, rows), :] = high[:, own].T
    turned[pl.ds(rows, rows), :] = low[:, own].T

    def step(t, carry):
        here = pl.ds(pl.multiple_of(t * tile, tile), tile)
        part = dot(high[own, :], high[here, :], NT)
        part += dot(low[own, :], high[here, :], NT)
        part += dot(high[own, :], low[here, :], NT)
        left_out[:, here] = DECAY_RATE * left_ref[:, here] + (1.0 - DECAY_RATE) * part
        both = dot(turned[...], high[:, here], NN)
        part = both[:rows] + both[rows:] + dot(turned[pl.ds(0, rows), :], low[:, here], NN)
        right_out[:, here] = DECAY_RATE * right_ref[:, here] + (1.0 - DECAY_RATE) * part
        return carry

    lax.fori_loop(0, size // tile, step, 0)


def stats(place, spread, left, right):
    rows, size = left.shape
    return pl.pallas_call(
        stats_kernel,
        out_shape=(jax.ShapeDtypeStruct(left.shape, left.dtype),) * 2,
        in_specs=[pl.BlockSpec(memory_space=pltpu.SMEM)] + [vmem()] * 3,
        out_specs=(vmem(),) * 2,
        scratch_shapes=[
            pltpu.VMEM((size, size), jnp.bfloat16),
            pltpu.VMEM((size, size), jnp.bfloat16),
            pltpu.VMEM((2 * rows, size), jnp.bfloat16),
        ],
        compiler_params=pltpu.CompilerParams(vmem_limit_bytes=24 * MIB),
        cost_estimate=cost(12 * size * size * rows, 6 * size * size),
        name="stats",
    )(place, spread, left, right)


def codes_of(value):
    rest = jnp.abs(value)
    depth = jnp.zeros(value.shape, jnp.float32)
    for bit in BITS:
        scaled = rest * (2.0**bit)
        keep = scaled < 4.0
        rest = jnp.where(keep, scaled, rest)
        depth = jnp.where(keep, depth + bit, depth)
    code = jnp.where(value == 0.0, 0.0, depth * 128.0 + rest * 64.0 - 127.0)
    return jnp.where(value < 0.0, -code, code).astype(jnp.int32).astype(jnp.int16)


def encode_kernel(place_ref, left_ref, code_ref):
    size = left_ref.shape[0]
    slabs = left_ref.shape[1] // size
    half = slabs // 2
    middle = size // 2

    def block(d):
        column = lax.rem(place_ref[0] + d, slabs) * size
        return left_ref[:, pl.ds(pl.multiple_of(column, size), size)].astype(jnp.float32)

    own = block(0)
    upper, corner = own[:middle], pltpu.roll(own[middle:], middle, 1)
    row = lax.broadcasted_iota(jnp.int32, upper.shape, 0)
    lane = lax.broadcasted_iota(jnp.int32, upper.shape, 1)
    diagonal = jnp.sum(jnp.where(row == lane, corner, 0.0), axis=0, keepdims=True)
    code_ref[pl.ds(0, HEAD), :] = codes_of(jnp.broadcast_to(diagonal, (HEAD, size)))
    code_ref[pl.ds(HEAD, middle), :] = codes_of(jnp.where((lane < middle) & (row > lane), corner, upper))
    start = HEAD + middle
    for d in range(1, half):
        code_ref[pl.ds(start, size), :] = codes_of(block(d))
        start += size
    last = block(half)
    last = jnp.where(place_ref[0] < half, last[:middle], last.T[middle:])
    code_ref[pl.ds(start, middle), :] = codes_of(last)


def encode(place, left, slabs):
    rows = left.shape[0]
    count = HEAD + slabs * rows // 2
    return pl.pallas_call(
        encode_kernel,
        out_shape=jax.ShapeDtypeStruct((count, rows), jnp.int16),
        in_specs=[pl.BlockSpec(memory_space=pltpu.SMEM), vmem()],
        out_specs=vmem(),
        compiler_params=pltpu.CompilerParams(vmem_limit_bytes=8 * MIB),
        cost_estimate=cost(30 * count * rows, 4 * left.size),
        name="encode",
    )(place, left)


def body(grads, assign, left_factor, right_factor, left_root, right_root):
    fsdp_size = lax.axis_size("fsdp")
    dp_size = lax.axis_size("dp")
    shard_rows = grads.shape[2]
    width = grads.shape[3]
    col_width = width // dp_size
    place = lax.axis_index("dp").astype(jnp.int32).reshape(1)
    outgoing = send(assign, grads[0], dp_size)
    outgoing = outgoing.reshape(fsdp_size * dp_size, shard_rows, col_width)
    outgoing, left_rows = lax.optimization_barrier((outgoing, left_root[0]))
    codes = encode(place, left_rows, dp_size)
    arrived = lax.all_to_all(outgoing, ("fsdp", "dp"), split_axis=0, concat_axis=0, tiled=True)
    packed, square = fold(arrived.reshape(fsdp_size, dp_size, shard_rows, col_width), codes)
    spread = lax.all_gather(packed, "dp", axis=0)
    shaped, squares = shape(spread, right_root[0], square)
    squares = lax.all_to_all(squares, "dp", split_axis=0, concat_axis=0, tiled=True)
    rounded = graft(squares, shaped).reshape(fsdp_size, shard_rows, col_width)
    rounded, spread = lax.optimization_barrier((rounded, spread))
    returned = lax.all_to_all(rounded, "fsdp", split_axis=0, concat_axis=0, tiled=True)
    left_out, right_out = stats(place, spread, left_factor[0], right_factor[0])
    update = place_blocks(assign, returned)
    return (update, left_out[None], right_out[None])


def solution(mesh):
    placed = (
        P("dp", None, "fsdp", None),
        P(),
        P("fsdp", "dp", None),
        P("fsdp", "dp", None),
        P("fsdp", "dp", None),
        P("fsdp", "dp", None),
    )
    return jax.shard_map(
        body,
        mesh=mesh,
        in_specs=placed,
        out_specs=(P(None, "fsdp", "dp"), P("fsdp", "dp", None), P("fsdp", "dp", None)),
        check_vma=False,
    )
```

```python
import functools

import jax
import jax.numpy as jnp
from jax import lax
from jax.experimental import pallas as pl
from jax.experimental.pallas import tpu as pltpu
from jax.sharding import PartitionSpec as P

DECAY_RATE = 0.999
EPSILON = 1e-06
STEPS = 90.0
TOP = 32767.0
FLOOR = 1e-30
CODES = 8
HEAD = 16
BITS = (64, 32, 16, 8, 4, 2, 1)
MIB = 1 << 20


def vmem():
    return pl.BlockSpec(memory_space=pltpu.VMEM)


def anywhere():
    return pl.BlockSpec(memory_space=pl.ANY)


def cost(flops, moved):
    return pl.CostEstimate(flops=flops, bytes_accessed=moved, transcendentals=0)


def send_kernel(dp_size, assign_ref, grads_ref, out_ref, owner_of, held, turned, assign_sem, in_sems, out_sem):
    blocks = grads_ref.shape[0]
    col_width = grads_ref.shape[2] // dp_size
    chunks = in_sems.shape[0]
    chunk = blocks // chunks
    loads = [
        pltpu.make_async_copy(
            grads_ref.at[pl.ds(c * chunk, chunk)], held.at[pl.ds(c * chunk, chunk)], in_sems.at[c]
        )
        for c in range(chunks)
    ]
    owners = pltpu.make_async_copy(assign_ref, owner_of, assign_sem)
    owners.start()
    for load in loads:
        load.start()
    owners.wait()
    for c in range(chunks):
        loads[c].wait()
        for b in range(c * chunk, (c + 1) * chunk):
            for k in range(dp_size):
                turned[b, k] = held[b, :, pl.ds(k * col_width, col_width)]
            pltpu.make_async_copy(turned.at[b], out_ref.at[owner_of[b]], out_sem).start()
    pltpu.make_async_copy(turned, out_ref, out_sem).wait()


def send(assign, grads, dp_size):
    blocks, rows, width = grads.shape
    shape = (blocks, dp_size, rows, width // dp_size)
    return pl.pallas_call(
        functools.partial(send_kernel, dp_size),
        out_shape=jax.ShapeDtypeStruct(shape, grads.dtype),
        in_specs=[anywhere()] * 2,
        out_specs=anywhere(),
        scratch_shapes=[
            pltpu.SMEM((blocks,), jnp.int32),
            pltpu.VMEM(grads.shape, grads.dtype),
            pltpu.VMEM(shape, grads.dtype),
            pltpu.SemaphoreType.DMA,
            pltpu.SemaphoreType.DMA((8,)),
            pltpu.SemaphoreType.DMA,
        ],
        compiler_params=pltpu.CompilerParams(vmem_limit_bytes=60 * MIB),
        cost_estimate=cost(0, 2 * grads.size * 2),
        name="send",
    )(assign, grads)


def scale_of(code):
    return jnp.exp(code * (1.0 / STEPS)) * (1.0 / TOP)


def fold_kernel(arrived_ref, root_ref, packed_ref, square_ref):
    shards, replicas, rows, width = arrived_ref.shape
    group = shards // CODES
    codes = []
    square = jnp.zeros((8, width), jnp.float32)
    for g in range(CODES):
        terms = arrived_ref[pl.ds(g * group, group)].astype(jnp.float32)
        total = jnp.sum(terms, axis=1).reshape(group * rows, width)
        peak = jnp.maximum(jnp.max(jnp.abs(total), axis=0, keepdims=True), FLOOR)
        code = jnp.ceil(jnp.log(peak) * STEPS)
        units = jnp.floor(total * (1.0 / scale_of(code)) + 0.5)
        units = jnp.clip(units, -TOP, TOP).astype(jnp.int32).astype(jnp.int16)
        packed_ref[pl.ds(g * group * rows, group * rows), :] = units
        codes.append(code)
        square = square + jnp.sum((total * total).reshape(group * rows // 8, 8, width), axis=0)
    square_ref[...] = square
    codes = [code.astype(jnp.int32) for code in codes] + [root_ref[pl.ds(0, HEAD), :].astype(jnp.int32)[CODES:]]
    size = shards * rows
    packed_ref[pl.ds(size, HEAD), :] = jnp.concatenate(codes, axis=0).astype(jnp.int16)
    rest = root_ref.shape[0] - HEAD
    packed_ref[pl.ds(size + HEAD, rest), :] = root_ref[pl.ds(HEAD, rest), :]


def fold(arrived, root):
    shards, replicas, rows, width = arrived.shape
    return pl.pallas_call(
        fold_kernel,
        out_shape=(
            jax.ShapeDtypeStruct((shards * rows + root.shape[0], width), jnp.int16),
            jax.ShapeDtypeStruct((8, width), jnp.float32),
        ),
        in_specs=[vmem()] * 2,
        out_specs=(vmem(),) * 2,
        compiler_params=pltpu.CompilerParams(vmem_limit_bytes=16 * MIB),
        cost_estimate=cost(arrived.size, 2 * arrived.size),
        name="fold",
    )(arrived, root)


def unpack(spread_ref, k, high, low, first, count):
    width = spread_ref.shape[2]
    size = high.shape[0]
    rows = size // CODES
    columns = pl.ds(k * width, width)
    scales = scale_of(spread_ref[k, pl.ds(size, HEAD), :].astype(jnp.int32)[:CODES].astype(jnp.float32))
    for g in range(first // rows, (first + count) // rows):
        here = pl.ds(g * rows, rows)
        units = spread_ref[k, here, :].astype(jnp.int32).astype(jnp.float32)
        values = units * scales[g : g + 1]
        upper = values.astype(jnp.bfloat16)
        high[here, columns] = upper
        low[here, columns] = (values - upper.astype(jnp.float32)).astype(jnp.bfloat16)


def values_of(code):
    code = code.astype(jnp.int32)
    power = jnp.exp2((1 - (code & 127)).astype(jnp.float32))
    return lax.shift_right_arithmetic(code, 7).astype(jnp.float32) * (1.0 / 128.0) * power


def decode(spread_ref, i, left):
    slabs, _, size = spread_ref.shape
    half = slabs // 2
    middle = size // 2
    head = left.shape[0]
    start = head + HEAD

    def at(a, b):
        return pl.ds(a * size, size), pl.ds(b * size, size)

    part = values_of(spread_ref[i, pl.ds(start, middle), :])
    corner = values_of(spread_ref[i, pl.ds(head, HEAD), :].astype(jnp.int32)[CODES : CODES + 1])
    both = jnp.concatenate([part, pltpu.roll(part, middle, 1)], axis=0)
    row = lax.broadcasted_iota(jnp.int32, both.shape, 0)
    lane = lax.broadcasted_iota(jnp.int32, both.shape, 1)
    direct = ((row < middle) & (row <= lane)) | ((row >= middle) & (lane >= middle) & (row > lane))
    value = jnp.where(direct, both, both.T)
    value = jnp.where((row == lane) & (row >= middle), pltpu.roll(corner, middle, 1), value)
    left[at(i, i)] = value.astype(jnp.bfloat16)
    start += middle
    for d in range(1, half):
        value = values_of(spread_ref[i, pl.ds(start, size), :]).astype(jnp.bfloat16)
        j = (i + d) % slabs
        left[at(i, j)] = value
        left[at(j, i)] = value.T
        start += size
    if i < half:
        rest = pl.ds(start, middle)
        value = values_of(jnp.concatenate([spread_ref[i, rest, :], spread_ref[i + half, rest, :]], axis=0))
        value = value.astype(jnp.bfloat16)
        left[at(i, i + half)] = value
        left[at(i + half, i)] = value.T


NT = (((1,), (1,)), ((), ()))
NN = (((1,), (0,)), ((), ()))


def dot(a, b, dims):
    return lax.dot_general(a, b, dims, preferred_element_type=jnp.float32)


def halves(a, b):
    a, b = (jnp.sum(x, axis=0, keepdims=True) for x in (a, b))
    width = a.shape[1]
    lane = lax.broadcasted_iota(jnp.int32, a.shape, 1)
    a, b = (x + pltpu.roll(x, width // 2, 1) for x in (a, b))
    return jnp.where(lane < width // 2, a, b)


def shape_kernel(spread_ref, right_ref, square_ref, out_ref, squares_ref, high, low, mid, left_ref):
    slabs = spread_ref.shape[0]
    size, width = out_ref.shape
    tile = 512
    for t in range(size // tile):
        rows = pl.ds(t * tile, tile)
        for k in range(slabs):
            unpack(spread_ref, k, high, low, t * tile, tile)
        for i in range(4 * t, 4 * t + 4):
            decode(spread_ref, i, left_ref)
        part = dot(high[rows, :], right_ref[...], NT) + dot(low[rows, :], right_ref[...], NT)
        upper = part.astype(jnp.bfloat16)
        mid[rows, pl.ds(0, width)] = upper
        mid[rows, pl.ds(width, width)] = (part - upper.astype(jnp.float32)).astype(jnp.bfloat16)

    square = jnp.zeros((8, width), jnp.float32)
    for t in range(size // tile):
        both = dot(left_ref[pl.ds(t * tile, tile), :], mid[...], NN)
        part = both[:, :width] + both[:, width:]
        square = square + jnp.sum((part * part).reshape(tile // 8, 8, width), axis=0)
        out_ref[pl.ds(t * tile, tile), :] = part
    squares_ref[...] = jnp.broadcast_to(halves(square, square_ref[...]), (slabs, width))


def shape(spread, right, square):
    slabs, _, width = spread.shape
    size = right.shape[1]
    return pl.pallas_call(
        shape_kernel,
        out_shape=(
            jax.ShapeDtypeStruct((size, width), jnp.float32),
            jax.ShapeDtypeStruct((slabs, width), jnp.float32),
        ),
        in_specs=[vmem()] * 3,
        out_specs=(vmem(),) * 2,
        scratch_shapes=[
            pltpu.VMEM((size, size), jnp.bfloat16),
            pltpu.VMEM((size, size), jnp.bfloat16),
            pltpu.VMEM((size, 2 * width), jnp.bfloat16),
            pltpu.VMEM((size, size), jnp.bfloat16),
        ],
        compiler_params=pltpu.CompilerParams(vmem_limit_bytes=24 * MIB),
        cost_estimate=cost(8 * size * size * width, 6 * size * size),
        name="shape",
    )(spread, right, square)


def graft_kernel(squares_ref, shaped_ref, out_ref):
    total = jnp.sum(squares_ref[...], axis=0, keepdims=True)
    first = lax.broadcasted_iota(jnp.int32, total.shape, 1) < total.shape[1] // 2
    shaped_square = jnp.sum(jnp.where(first, total, 0.0), axis=1, keepdims=True)
    block_square = jnp.sum(jnp.where(first, 0.0, total), axis=1, keepdims=True)
    ratio = jnp.sqrt((block_square + EPSILON) / (shaped_square + EPSILON))
    out_ref[...] = (shaped_ref[...] * ratio).astype(jnp.bfloat16)


def graft(squares, shaped):
    return pl.pallas_call(
        graft_kernel,
        out_shape=jax.ShapeDtypeStruct(shaped.shape, jnp.bfloat16),
        in_specs=[vmem()] * 2,
        out_specs=vmem(),
        compiler_params=pltpu.CompilerParams(vmem_limit_bytes=8 * MIB),
        cost_estimate=cost(shaped.size, 6 * shaped.size),
        name="graft",
    )(squares, shaped)


def place_kernel(assign_ref, returned_ref, out_ref):
    for b in range(out_ref.shape[0]):
        out_ref[b] = returned_ref[assign_ref[b]]


def place_blocks(assign, returned):
    return pl.pallas_call(
        place_kernel,
        out_shape=jax.ShapeDtypeStruct(returned.shape, returned.dtype),
        in_specs=[pl.BlockSpec(memory_space=pltpu.SMEM), vmem()],
        out_specs=vmem(),
        compiler_params=pltpu.CompilerParams(vmem_limit_bytes=8 * MIB),
        cost_estimate=cost(0, 4 * returned.size),
        name="place",
    )(assign, returned)


def stats_kernel(place_ref, spread_ref, left_ref, right_ref, left_out, right_out, high, low, turned):
    slabs = spread_ref.shape[0]
    rows, size = left_ref.shape
    tile = 256
    for t in range(size // tile):
        for k in range(slabs):
            unpack(spread_ref, k, high, low, t * tile, tile)
    own = pl.ds(pl.multiple_of(place_ref[0] * rows, rows), rows)
    turned[pl.ds(0, rows), :] = high[:, own].T
    turned[pl.ds(rows, rows), :] = low[:, own].T

    mine = jnp.concatenate([high[own, :], low[own, :]], axis=0)
    for t in range(size // tile):
        here = pl.ds(t * tile, tile)
        both = dot(high[here, :], mine, NT)
        part = both[:, :rows] + both[:, rows:] + dot(low[here, :], mine[:rows], NT)
        left_out[:, here] = DECAY_RATE * left_ref[:, here] + (1.0 - DECAY_RATE) * part.T
        both = dot(turned[...], high[:, here], NN)
        part = both[:rows] + both[rows:] + dot(turned[pl.ds(0, rows), :], low[:, here], NN)
        right_out[:, here] = DECAY_RATE * right_ref[:, here] + (1.0 - DECAY_RATE) * part


def stats(place, spread, left, right):
    rows, size = left.shape
    return pl.pallas_call(
        stats_kernel,
        out_shape=(jax.ShapeDtypeStruct(left.shape, left.dtype),) * 2,
        in_specs=[pl.BlockSpec(memory_space=pltpu.SMEM)] + [vmem()] * 3,
        out_specs=(vmem(),) * 2,
        scratch_shapes=[
            pltpu.VMEM((size, size), jnp.bfloat16),
            pltpu.VMEM((size, size), jnp.bfloat16),
            pltpu.VMEM((2 * rows, size), jnp.bfloat16),
        ],
        compiler_params=pltpu.CompilerParams(vmem_limit_bytes=24 * MIB),
        cost_estimate=cost(12 * size * size * rows, 6 * size * size),
        name="stats",
    )(place, spread, left, right)


def codes_of(value):
    rest = jnp.abs(value)
    depth = jnp.zeros(value.shape, jnp.float32)
    for bit in BITS:
        scaled = rest * (2.0**bit)
        keep = scaled < 4.0
        rest = jnp.where(keep, scaled, rest)
        depth = jnp.where(keep, depth + bit, depth)
    fraction = jnp.where(value < 0.0, -rest, rest) * 64.0
    return (fraction * 128.0 + depth).astype(jnp.int32).astype(jnp.int16)


def encode_kernel(place_ref, left_ref, code_ref):
    size = left_ref.shape[0]
    slabs = left_ref.shape[1] // size
    half = slabs // 2
    middle = size // 2

    def block(d):
        column = lax.rem(place_ref[0] + d, slabs) * size
        return left_ref[:, pl.ds(pl.multiple_of(column, size), size)].astype(jnp.float32)

    own = block(0)
    upper, corner = own[:middle], pltpu.roll(own[middle:], middle, 1)
    row = lax.broadcasted_iota(jnp.int32, upper.shape, 0)
    lane = lax.broadcasted_iota(jnp.int32, upper.shape, 1)
    diagonal = jnp.sum(jnp.where(row == lane, corner, 0.0), axis=0, keepdims=True)
    code_ref[pl.ds(0, HEAD), :] = codes_of(jnp.broadcast_to(diagonal, (HEAD, size)))
    code_ref[pl.ds(HEAD, middle), :] = codes_of(jnp.where((lane < middle) & (row > lane), corner, upper))
    start = HEAD + middle
    for d in range(1, half):
        code_ref[pl.ds(start, size), :] = codes_of(block(d))
        start += size
    last = block(half)
    last = jnp.where(place_ref[0] < half, last[:middle], last.T[middle:])
    code_ref[pl.ds(start, middle), :] = codes_of(last)


def encode(place, left, slabs):
    rows = left.shape[0]
    count = HEAD + slabs * rows // 2
    return pl.pallas_call(
        encode_kernel,
        out_shape=jax.ShapeDtypeStruct((count, rows), jnp.int16),
        in_specs=[pl.BlockSpec(memory_space=pltpu.SMEM), vmem()],
        out_specs=vmem(),
        compiler_params=pltpu.CompilerParams(vmem_limit_bytes=8 * MIB),
        cost_estimate=cost(30 * count * rows, 4 * left.size),
        name="encode",
    )(place, left)


def body(grads, assign, left_factor, right_factor, left_root, right_root):
    fsdp_size = lax.axis_size("fsdp")
    dp_size = lax.axis_size("dp")
    shard_rows = grads.shape[2]
    width = grads.shape[3]
    col_width = width // dp_size
    place = lax.axis_index("dp").astype(jnp.int32).reshape(1)
    outgoing = send(assign, grads[0], dp_size)
    outgoing = outgoing.reshape(fsdp_size * dp_size, shard_rows, col_width)
    outgoing, left_rows = lax.optimization_barrier((outgoing, left_root[0]))
    codes = encode(place, left_rows, dp_size)
    arrived = lax.all_to_all(outgoing, ("fsdp", "dp"), split_axis=0, concat_axis=0, tiled=True)
    packed, square = fold(arrived.reshape(fsdp_size, dp_size, shard_rows, col_width), codes)
    spread = lax.all_gather(packed, "dp", axis=0)
    shaped, squares = shape(spread, right_root[0], square)
    squares = lax.all_to_all(squares, "dp", split_axis=0, concat_axis=0, tiled=True)
    rounded = graft(squares, shaped).reshape(fsdp_size, shard_rows, col_width)
    rounded, spread = lax.optimization_barrier((rounded, spread))
    returned = lax.all_to_all(rounded, "fsdp", split_axis=0, concat_axis=0, tiled=True)
    left_out, right_out = stats(place, spread, left_factor[0], right_factor[0])
    update = place_blocks(assign, returned)
    return (update, left_out[None], right_out[None])


def solution(mesh):
    placed = (
        P("dp", None, "fsdp", None),
        P(),
        P("fsdp", "dp", None),
        P("fsdp", "dp", None),
        P("fsdp", "dp", None),
        P("fsdp", "dp", None),
    )
    return jax.shard_map(
        body,
        mesh=mesh,
        in_specs=placed,
        out_specs=(P(None, "fsdp", "dp"), P("fsdp", "dp", None), P("fsdp", "dp", None)),
        check_vma=False,
    )
```

```python
import functools

import jax
import jax.numpy as jnp
from jax import lax
from jax.experimental import pallas as pl
from jax.experimental.pallas import tpu as pltpu
from jax.sharding import PartitionSpec as P

DECAY_RATE = 0.999
EPSILON = 1e-06
STEPS = 90.0
TOP = 32767.0
FLOOR = 1e-30
CODES = 8
HEAD = 16
BITS = (64, 32, 16, 8, 4, 2, 1)
MIB = 1 << 20


def vmem():
    return pl.BlockSpec(memory_space=pltpu.VMEM)


def anywhere():
    return pl.BlockSpec(memory_space=pl.ANY)


def cost(flops, moved):
    return pl.CostEstimate(flops=flops, bytes_accessed=moved, transcendentals=0)


def send_kernel(dp_size, assign_ref, grads_ref, out_ref, owner_of, held, turned, assign_sem, in_sems, out_sem):
    blocks = grads_ref.shape[0]
    col_width = grads_ref.shape[2] // dp_size
    chunks = in_sems.shape[0]
    chunk = blocks // chunks
    loads = [
        pltpu.make_async_copy(
            grads_ref.at[pl.ds(c * chunk, chunk)], held.at[pl.ds(c * chunk, chunk)], in_sems.at[c]
        )
        for c in range(chunks)
    ]
    owners = pltpu.make_async_copy(assign_ref, owner_of, assign_sem)
    owners.start()
    for load in loads:
        load.start()
    owners.wait()
    for c in range(chunks):
        loads[c].wait()
        for b in range(c * chunk, (c + 1) * chunk):
            for k in range(dp_size):
                turned[b, k] = held[b, :, pl.ds(k * col_width, col_width)]
            pltpu.make_async_copy(turned.at[b], out_ref.at[owner_of[b]], out_sem).start()
    pltpu.make_async_copy(turned, out_ref, out_sem).wait()


def send(assign, grads, dp_size):
    blocks, rows, width = grads.shape
    shape = (blocks, dp_size, rows, width // dp_size)
    return pl.pallas_call(
        functools.partial(send_kernel, dp_size),
        out_shape=jax.ShapeDtypeStruct(shape, grads.dtype),
        in_specs=[anywhere()] * 2,
        out_specs=anywhere(),
        scratch_shapes=[
            pltpu.SMEM((blocks,), jnp.int32),
            pltpu.VMEM(grads.shape, grads.dtype),
            pltpu.VMEM(shape, grads.dtype),
            pltpu.SemaphoreType.DMA,
            pltpu.SemaphoreType.DMA((8,)),
            pltpu.SemaphoreType.DMA,
        ],
        compiler_params=pltpu.CompilerParams(vmem_limit_bytes=60 * MIB),
        cost_estimate=cost(0, 2 * grads.size * 2),
        name="send",
    )(assign, grads)


def scale_of(code):
    return jnp.exp(code * (1.0 / STEPS)) * (1.0 / TOP)


def fold_kernel(arrived_ref, root_ref, packed_ref, square_ref):
    shards, replicas, rows, width = arrived_ref.shape
    group = shards // CODES
    codes = []
    square = jnp.zeros((8, width), jnp.float32)
    for g in range(CODES):
        terms = arrived_ref[pl.ds(g * group, group)].astype(jnp.float32)
        total = jnp.sum(terms, axis=1).reshape(group * rows, width)
        peak = jnp.maximum(jnp.max(jnp.abs(total), axis=0, keepdims=True), FLOOR)
        code = jnp.ceil(jnp.log(peak) * STEPS)
        units = jnp.floor(total * (1.0 / scale_of(code)) + 0.5)
        units = jnp.clip(units, -TOP, TOP).astype(jnp.int32).astype(jnp.int16)
        packed_ref[pl.ds(g * group * rows, group * rows), :] = units
        codes.append(code)
        square = square + jnp.sum((total * total).reshape(group * rows // 8, 8, width), axis=0)
    square_ref[...] = square
    codes = [code.astype(jnp.int32) for code in codes] + [root_ref[pl.ds(0, HEAD), :].astype(jnp.int32)[CODES:]]
    size = shards * rows
    packed_ref[pl.ds(size, HEAD), :] = jnp.concatenate(codes, axis=0).astype(jnp.int16)
    rest = root_ref.shape[0] - HEAD
    packed_ref[pl.ds(size + HEAD, rest), :] = root_ref[pl.ds(HEAD, rest), :]


def fold(arrived, root):
    shards, replicas, rows, width = arrived.shape
    return pl.pallas_call(
        fold_kernel,
        out_shape=(
            jax.ShapeDtypeStruct((shards * rows + root.shape[0], width), jnp.int16),
            jax.ShapeDtypeStruct((8, width), jnp.float32),
        ),
        in_specs=[vmem()] * 2,
        out_specs=(vmem(),) * 2,
        compiler_params=pltpu.CompilerParams(vmem_limit_bytes=16 * MIB),
        cost_estimate=cost(arrived.size, 2 * arrived.size),
        name="fold",
    )(arrived, root)


def halves_of(spread_ref, k, size, first, count):
    rows = size // CODES
    scales = scale_of(spread_ref[k, pl.ds(size, HEAD), :].astype(jnp.int32)[:CODES].astype(jnp.float32))
    upper, lower = [], []
    for g in range(first // rows, (first + count) // rows):
        units = spread_ref[k, pl.ds(g * rows, rows), :].astype(jnp.int32).astype(jnp.float32)
        values = units * scales[g : g + 1]
        upper.append(values.astype(jnp.bfloat16))
        lower.append((values - upper[-1].astype(jnp.float32)).astype(jnp.bfloat16))
    return jnp.concatenate(upper, axis=0), jnp.concatenate(lower, axis=0)


def unpack(spread_ref, k, high, low, first, count):
    width = spread_ref.shape[2]
    here = pl.ds(first, count), pl.ds(k * width, width)
    high[here], low[here] = halves_of(spread_ref, k, high.shape[0], first, count)


def values_of(code):
    code = code.astype(jnp.int32)
    power = jnp.exp2((1 - (code & 127)).astype(jnp.float32))
    return lax.shift_right_arithmetic(code, 7).astype(jnp.float32) * (1.0 / 128.0) * power


def decode(spread_ref, i, left):
    slabs, _, size = spread_ref.shape
    half = slabs // 2
    middle = size // 2
    head = left.shape[0]
    start = head + HEAD

    def at(a, b):
        return pl.ds(a * size, size), pl.ds(b * size, size)

    part = values_of(spread_ref[i, pl.ds(start, middle), :])
    corner = values_of(spread_ref[i, pl.ds(head, HEAD), :].astype(jnp.int32)[CODES : CODES + 1])
    both = jnp.concatenate([part, pltpu.roll(part, middle, 1)], axis=0)
    row = lax.broadcasted_iota(jnp.int32, both.shape, 0)
    lane = lax.broadcasted_iota(jnp.int32, both.shape, 1)
    direct = ((row < middle) & (row <= lane)) | ((row >= middle) & (lane >= middle) & (row > lane))
    value = jnp.where(direct, both, both.T)
    value = jnp.where((row == lane) & (row >= middle), pltpu.roll(corner, middle, 1), value)
    left[at(i, i)] = value.astype(jnp.bfloat16)
    start += middle
    for d in range(1, half):
        value = values_of(spread_ref[i, pl.ds(start, size), :]).astype(jnp.bfloat16)
        j = (i + d) % slabs
        left[at(i, j)] = value
        left[at(j, i)] = value.T
        start += size
    if i < half:
        rest = pl.ds(start, middle)
        value = values_of(jnp.concatenate([spread_ref[i, rest, :], spread_ref[i + half, rest, :]], axis=0))
        value = value.astype(jnp.bfloat16)
        left[at(i, i + half)] = value
        left[at(i + half, i)] = value.T


NT = (((1,), (1,)), ((), ()))
NN = (((1,), (0,)), ((), ()))


def dot(a, b, dims):
    return lax.dot_general(a, b, dims, preferred_element_type=jnp.float32)


def halves(a, b):
    a, b = (jnp.sum(x, axis=0, keepdims=True) for x in (a, b))
    width = a.shape[1]
    lane = lax.broadcasted_iota(jnp.int32, a.shape, 1)
    a, b = (x + pltpu.roll(x, width // 2, 1) for x in (a, b))
    return jnp.where(lane < width // 2, a, b)


def shape_kernel(spread_ref, right_ref, square_ref, out_ref, squares_ref, mid, left_ref):
    slabs = spread_ref.shape[0]
    size, width = out_ref.shape
    tile = 256
    for t in range(size // tile):
        rows = pl.ds(t * tile, tile)
        pairs = [halves_of(spread_ref, k, size, t * tile, tile) for k in range(slabs)]
        upper, lower = (jnp.concatenate(terms, axis=1) for terms in zip(*pairs))
        for i in range(2 * t, 2 * t + 2):
            decode(spread_ref, i, left_ref)
        part = dot(upper, right_ref[...], NT) + dot(lower, right_ref[...], NT)
        upper = part.astype(jnp.bfloat16)
        mid[rows, pl.ds(0, width)] = upper
        mid[rows, pl.ds(width, width)] = (part - upper.astype(jnp.float32)).astype(jnp.bfloat16)

    square = jnp.zeros((8, width), jnp.float32)
    for t in range(size // tile):
        both = dot(left_ref[pl.ds(t * tile, tile), :], mid[...], NN)
        part = both[:, :width] + both[:, width:]
        square = square + jnp.sum((part * part).reshape(tile // 8, 8, width), axis=0)
        out_ref[pl.ds(t * tile, tile), :] = part
    squares_ref[...] = jnp.broadcast_to(halves(square, square_ref[...]), (slabs, width))


def shape(spread, right, square):
    slabs, _, width = spread.shape
    size = right.shape[1]
    return pl.pallas_call(
        shape_kernel,
        out_shape=(
            jax.ShapeDtypeStruct((size, width), jnp.float32),
            jax.ShapeDtypeStruct((slabs, width), jnp.float32),
        ),
        in_specs=[vmem()] * 3,
        out_specs=(vmem(),) * 2,
        scratch_shapes=[
            pltpu.VMEM((size, 2 * width), jnp.bfloat16),
            pltpu.VMEM((size, size), jnp.bfloat16),
        ],
        compiler_params=pltpu.CompilerParams(vmem_limit_bytes=24 * MIB),
        cost_estimate=cost(8 * size * size * width, 6 * size * size),
        name="shape",
    )(spread, right, square)


def graft_kernel(squares_ref, shaped_ref, out_ref):
    total = jnp.sum(squares_ref[...], axis=0, keepdims=True)
    first = lax.broadcasted_iota(jnp.int32, total.shape, 1) < total.shape[1] // 2
    shaped_square = jnp.sum(jnp.where(first, total, 0.0), axis=1, keepdims=True)
    block_square = jnp.sum(jnp.where(first, 0.0, total), axis=1, keepdims=True)
    ratio = jnp.sqrt((block_square + EPSILON) / (shaped_square + EPSILON))
    out_ref[...] = (shaped_ref[...] * ratio).astype(jnp.bfloat16)


def graft(squares, shaped):
    return pl.pallas_call(
        graft_kernel,
        out_shape=jax.ShapeDtypeStruct(shaped.shape, jnp.bfloat16),
        in_specs=[vmem()] * 2,
        out_specs=vmem(),
        compiler_params=pltpu.CompilerParams(vmem_limit_bytes=8 * MIB),
        cost_estimate=cost(shaped.size, 6 * shaped.size),
        name="graft",
    )(squares, shaped)


def place_kernel(assign_ref, returned_ref, out_ref):
    for b in range(out_ref.shape[0]):
        out_ref[b] = returned_ref[assign_ref[b]]


def place_blocks(assign, returned):
    return pl.pallas_call(
        place_kernel,
        out_shape=jax.ShapeDtypeStruct(returned.shape, returned.dtype),
        in_specs=[pl.BlockSpec(memory_space=pltpu.SMEM), vmem()],
        out_specs=vmem(),
        compiler_params=pltpu.CompilerParams(vmem_limit_bytes=8 * MIB),
        cost_estimate=cost(0, 4 * returned.size),
        name="place",
    )(assign, returned)


def stats_kernel(place_ref, spread_ref, left_ref, right_ref, left_out, right_out, high, low, turned):
    slabs = spread_ref.shape[0]
    rows, size = left_ref.shape
    tile = 256
    for t in range(size // tile):
        for k in range(slabs):
            unpack(spread_ref, k, high, low, t * tile, tile)
    own = pl.ds(pl.multiple_of(place_ref[0] * rows, rows), rows)
    turned[pl.ds(0, rows), :] = high[:, own].T
    turned[pl.ds(rows, rows), :] = low[:, own].T

    mine = jnp.concatenate([high[own, :], low[own, :]], axis=0)
    for t in range(size // tile):
        here = pl.ds(t * tile, tile)
        both = dot(high[here, :], mine, NT)
        part = both[:, :rows] + both[:, rows:] + dot(low[here, :], mine[:rows], NT)
        left_out[:, here] = DECAY_RATE * left_ref[:, here] + (1.0 - DECAY_RATE) * part.T
        both = dot(turned[...], high[:, here], NN)
        part = both[:rows] + both[rows:] + dot(turned[pl.ds(0, rows), :], low[:, here], NN)
        right_out[:, here] = DECAY_RATE * right_ref[:, here] + (1.0 - DECAY_RATE) * part


def stats(place, spread, left, right):
    rows, size = left.shape
    return pl.pallas_call(
        stats_kernel,
        out_shape=(jax.ShapeDtypeStruct(left.shape, left.dtype),) * 2,
        in_specs=[pl.BlockSpec(memory_space=pltpu.SMEM)] + [vmem()] * 3,
        out_specs=(vmem(),) * 2,
        scratch_shapes=[
            pltpu.VMEM((size, size), jnp.bfloat16),
            pltpu.VMEM((size, size), jnp.bfloat16),
            pltpu.VMEM((2 * rows, size), jnp.bfloat16),
        ],
        compiler_params=pltpu.CompilerParams(vmem_limit_bytes=24 * MIB),
        cost_estimate=cost(12 * size * size * rows, 6 * size * size),
        name="stats",
    )(place, spread, left, right)


def codes_of(value):
    rest = jnp.abs(value)
    depth = jnp.zeros(value.shape, jnp.float32)
    for bit in BITS:
        scaled = rest * (2.0**bit)
        keep = scaled < 4.0
        rest = jnp.where(keep, scaled, rest)
        depth = jnp.where(keep, depth + bit, depth)
    fraction = jnp.where(value < 0.0, -rest, rest) * 64.0
    return (fraction * 128.0 + depth).astype(jnp.int32).astype(jnp.int16)


def encode_kernel(place_ref, left_ref, code_ref):
    size = left_ref.shape[0]
    slabs = left_ref.shape[1] // size
    half = slabs // 2
    middle = size // 2

    def block(d):
        column = lax.rem(place_ref[0] + d, slabs) * size
        return left_ref[:, pl.ds(pl.multiple_of(column, size), size)].astype(jnp.float32)

    own = block(0)
    upper, corner = own[:middle], pltpu.roll(own[middle:], middle, 1)
    row = lax.broadcasted_iota(jnp.int32, upper.shape, 0)
    lane = lax.broadcasted_iota(jnp.int32, upper.shape, 1)
    diagonal = jnp.sum(jnp.where(row == lane, corner, 0.0), axis=0, keepdims=True)
    code_ref[pl.ds(0, HEAD), :] = codes_of(jnp.broadcast_to(diagonal, (HEAD, size)))
    code_ref[pl.ds(HEAD, middle), :] = codes_of(jnp.where((lane < middle) & (row > lane), corner, upper))
    start = HEAD + middle
    for d in range(1, half):
        code_ref[pl.ds(start, size), :] = codes_of(block(d))
        start += size
    last = block(half)
    last = jnp.where(place_ref[0] < half, last[:middle], last.T[middle:])
    code_ref[pl.ds(start, middle), :] = codes_of(last)


def encode(place, left, slabs):
    rows = left.shape[0]
    count = HEAD + slabs * rows // 2
    return pl.pallas_call(
        encode_kernel,
        out_shape=jax.ShapeDtypeStruct((count, rows), jnp.int16),
        in_specs=[pl.BlockSpec(memory_space=pltpu.SMEM), vmem()],
        out_specs=vmem(),
        compiler_params=pltpu.CompilerParams(vmem_limit_bytes=8 * MIB),
        cost_estimate=cost(30 * count * rows, 4 * left.size),
        name="encode",
    )(place, left)


def body(grads, assign, left_factor, right_factor, left_root, right_root):
    fsdp_size = lax.axis_size("fsdp")
    dp_size = lax.axis_size("dp")
    shard_rows = grads.shape[2]
    width = grads.shape[3]
    col_width = width // dp_size
    place = lax.axis_index("dp").astype(jnp.int32).reshape(1)
    outgoing = send(assign, grads[0], dp_size)
    outgoing = outgoing.reshape(fsdp_size * dp_size, shard_rows, col_width)
    outgoing, left_rows = lax.optimization_barrier((outgoing, left_root[0]))
    codes = encode(place, left_rows, dp_size)
    arrived = lax.all_to_all(outgoing, ("fsdp", "dp"), split_axis=0, concat_axis=0, tiled=True)
    packed, square = fold(arrived.reshape(fsdp_size, dp_size, shard_rows, col_width), codes)
    spread = lax.all_gather(packed, "dp", axis=0)
    shaped, squares = shape(spread, right_root[0], square)
    squares = lax.all_to_all(squares, "dp", split_axis=0, concat_axis=0, tiled=True)
    rounded = graft(squares, shaped).reshape(fsdp_size, shard_rows, col_width)
    rounded, spread = lax.optimization_barrier((rounded, spread))
    returned = lax.all_to_all(rounded, "fsdp", split_axis=0, concat_axis=0, tiled=True)
    left_out, right_out = stats(place, spread, left_factor[0], right_factor[0])
    update = place_blocks(assign, returned)
    return (update, left_out[None], right_out[None])


def solution(mesh):
    placed = (
        P("dp", None, "fsdp", None),
        P(),
        P("fsdp", "dp", None),
        P("fsdp", "dp", None),
        P("fsdp", "dp", None),
        P("fsdp", "dp", None),
    )
    return jax.shard_map(
        body,
        mesh=mesh,
        in_specs=placed,
        out_specs=(P(None, "fsdp", "dp"), P("fsdp", "dp", None), P("fsdp", "dp", None)),
        check_vma=False,
    )
```
